32 devices in a mesh: view: 4 (over y, x), xy: 4 (over z), gz: 2 (over core).
Axes of the slice: x: 2, y: 2, z: 4, core: 2. Of those that a mesh axis runs over, the one named last changes fastest.
Arguments:
- estimate: float32 [64, 256, 128], P('gz', 'xy'), may hold values from 0.5 to 2
- views: bfloat16 [4, 64, 256, 128], P('view', 'gz', 'xy'), may hold values from 0.19921875 to 3
- shifts: int32 [4, 3], P('view'), may hold values from -32 to 32, as said below
- kernels: float32 [4, 3, 63], P('view'), may hold values from 0.02 to 1
- coverage: int32 [4, 2, 1], replicated, may hold values from 0 to 1, as said below
Outputs:
- refined: float32 [64, 256, 128], P('gz', 'xy')
The draws below stay inside these ranges and needn't reach their ends.
Inputs may be any that keep to these rules, and one draw needn't show every extreme that they name: `shifts`: both ends -32 and 32 occur in every draw. `coverage`: every block is covered by at least one view.
All inputs are finite; a program needn't handle non-finite values.
Results may differ from the reference program's by a relative error of at most 0.0003.
Values may be sent and summed in bfloat16 or wider, within the bound.
A program may use at most 64 MiB of HBM per device.

```python
import math
import jax
import jax.numpy as jnp
from jax import lax

TAPS = 63
SHIFT = 32
BLOCK = 128
ITERS = 2
NX = 128
VIEWS = 4
NZ = 64
NY = 256


def draw_shifts(key, part):
    values = jax.random.randint(key, (VIEWS, 3), -SHIFT, SHIFT + 1).reshape(-1)
    order = jax.random.permutation(jax.random.fold_in(key, 1), VIEWS * 3)
    values = values.at[order[0]].set(SHIFT)
    values = values.at[order[1]].set(-SHIFT)
    return values.reshape(VIEWS, 3).astype(jnp.int32)


def draw_coverage(key, part):
    shape = (VIEWS, NY // BLOCK, NX // BLOCK)
    picks = jax.random.randint(key, shape, 0, 5)
    covered = (picks < 3).astype(jnp.int32)
    forced = jax.random.randint(jax.random.fold_in(key, 7), (NY // BLOCK, NX // BLOCK), 0, VIEWS)
    chosen = (jnp.arange(VIEWS)[:, None, None] == forced[None]).astype(jnp.int32)
    return jnp.maximum(covered, chosen).astype(jnp.int32)


def block_scale(rng, shape, shards, least, top_value):
    def one(axis_at, parts):
        heights = jax.random.uniform(jax.random.fold_in(jax.random.fold_in(rng, 6), axis_at), (parts,), jnp.float32, least / len(shards), top_value / len(shards))
        return jnp.repeat(jnp.exp(heights), shape[axis_at] // parts).reshape((-1,) + (1,) * (len(shape) - axis_at - 1))

    gain = one(*shards[0])
    for cut in shards[1:]:
        gain = gain * one(*cut)
    return gain


def setup_inputs(seed: int = 0) -> dict:
    seeds = jax.random.split(jax.random.key(seed), 6)
    estimate = jnp.clip(0.5 + 1.5 * jax.random.uniform(seeds[0], (NZ, NY, NX), jnp.float32) ** block_scale(seeds[0], (NZ, NY, NX), ((0, 2), (1, 4)), -0.2, 0.2), 0.5, 2.0)
    views = jnp.clip(0.19921875 + 2.8007812 * jax.random.uniform(seeds[1], (VIEWS, NZ, NY, NX), jnp.float32) ** block_scale(seeds[1], (VIEWS, NZ, NY, NX), ((0, 4), (1, 2), (2, 4)), -0.2, 0.2), 0.19921875, 3.0).astype(jnp.bfloat16)
    shifts = draw_shifts(jax.random.fold_in(seeds[5], 71), 0)
    kernels = jnp.clip(jnp.exp(math.log(1.0) - 3.912023 * jax.random.uniform(seeds[3], (VIEWS, 3, TAPS), jnp.float32) ** block_scale(seeds[3], (VIEWS, 3, TAPS), ((0, 4),), -0.2, 0.2)), 0.02, 1.0)
    coverage = draw_coverage(jax.random.fold_in(seeds[5], 71), 0)
    return dict(estimate=estimate, views=views, shifts=shifts, kernels=kernels, coverage=coverage)


def filtered(vol, taps_row, axis):
    half = (TAPS - 1) // 2
    length = vol.shape[axis]
    total = length + TAPS - 1
    spectrum = jnp.fft.rfft(vol, n=total, axis=axis)
    kernel_hat = jnp.fft.rfft(taps_row, n=total)
    shape = [1, 1, 1]
    shape[axis] = kernel_hat.shape[0]
    full = jnp.fft.irfft(spectrum * kernel_hat.reshape(shape), n=total, axis=axis)
    return lax.slice_in_dim(full, half, half + length, axis=axis).astype(vol.dtype)


def separable(vol, psf_view, forward):
    result = vol
    for axis in (2, 1, 0):
        row = psf_view[axis]
        taps_row = row[::-1] if forward else row
        result = filtered(result, taps_row, axis)
    return result


def reference(estimate, views, shifts, kernels, coverage):
    psf = kernels / jnp.sum(kernels, axis=2, keepdims=True)
    weights = jnp.repeat(jnp.repeat(coverage.astype(jnp.float32), BLOCK, axis=1), BLOCK, axis=2)
    count = jnp.sum(weights, axis=0)
    data = []
    for view_id in range(VIEWS):
        padded = jnp.pad(views[view_id].astype(jnp.float32), SHIFT)
        start = (SHIFT + shifts[view_id]).astype(jnp.int32)
        data.append(lax.dynamic_slice(padded, (start[0], start[1], start[2]), (NZ, NY, NX)))
    field = estimate
    for step in range(ITERS):
        total = jnp.zeros_like(field)
        for view_id in range(VIEWS):
            predicted = separable(field, psf[view_id], True)
            ratio = data[view_id] / (predicted + 0.05)
            total = total + weights[view_id][None] * separable(ratio, psf[view_id], False)
        field = field * total / count[None]
    return field
```

```python
import jax
import jax.numpy as jnp
from jax import lax
from jax.sharding import PartitionSpec as P

SHIFT = 32
BLOCK = 128
ITERS = 2


def extended(cells, sides, width):
    for axis, dim in sides:
        count = lax.axis_size(axis)
        ends = count - 1
        head = lax.slice_in_dim(cells, 0, width, axis=dim)
        tail = lax.slice_in_dim(cells, cells.shape[dim] - width, cells.shape[dim], axis=dim)
        cells = jnp.concatenate(
            [
                lax.ppermute(tail, axis, [(i, (i + 1) % count) for i in range(ends)]),
                cells,
                lax.ppermute(head, axis, [((i + 1) % count, i) for i in range(ends)]),
            ],
            axis=dim,
        )
    return cells


def band(kern, rows, cols, offset):
    row_ids = lax.broadcasted_iota(jnp.int32, (rows, cols), 0)
    col_ids = lax.broadcasted_iota(jnp.int32, (rows, cols), 1)
    offsets = row_ids - col_ids + offset

    taps = kern.shape[0]
    tap_ids = lax.broadcasted_iota(jnp.int32, (taps, rows, cols), 0)
    return jnp.sum(jnp.where(offsets[None] == tap_ids, kern[:, None, None], 0.0), axis=0)


def along_x(vol, matrix):
    return jnp.einsum("zyx,xk->zyk", vol, matrix, precision=lax.Precision.HIGHEST)


def along_rows(vol, rim_mat, half):
    padded = extended(vol.astype(jnp.bfloat16), (("xy", 1),), half).astype(vol.dtype)
    return jnp.einsum("zyx,yk->zkx", padded, rim_mat, precision=lax.Precision.HIGHEST)


def along_planes(vol, matrix, half):
    padded = extended(vol, (("gz", 0),), half)
    return jnp.einsum("zyx,zk->kyx", padded, matrix, precision=lax.Precision.HIGHEST)


def on_device(estimate, views, shifts, kernels, coverage):
    slab, strip, width = estimate.shape
    taps = kernels.shape[2]
    half = (taps - 1) // 2
    psf = kernels[0] / jnp.sum(kernels[0], axis=1, keepdims=True)
    raw = views[0]
    margin = SHIFT
    padded = extended(raw, (("gz", 0), ("xy", 1)), margin)
    padded = jnp.pad(padded, ((0, 0), (0, 0), (margin, margin)))
    start = margin + shifts[0]
    data = lax.dynamic_slice(padded, (start[0], start[1], start[2]), (slab, strip, width)).astype(
        jnp.float32
    )
    field = estimate
    row_first = lax.axis_index("xy") * strip
    planes = field.shape[0]
    mats = []
    for reverse in (False, True):
        rows_psf = psf[:, ::-1] if reverse else psf
        x_mat = band(rows_psf[2], width, width, half)
        z_mat = band(rows_psf[0], planes + 2 * half, planes, 0)
        rim_mat = band(rows_psf[1], strip + 2 * half, strip, 0)
        mats.append((x_mat, None, rim_mat, z_mat))
    row_global = row_first + lax.broadcasted_iota(jnp.int32, (strip,), 0)
    row_onehot = (row_global[:, None] // BLOCK == jnp.arange(coverage.shape[1])[None]).astype(
        jnp.float32
    )
    col_onehot = (
        jnp.arange(width)[:, None] // BLOCK == jnp.arange(coverage.shape[2])[None]
    ).astype(jnp.float32)
    grid = jnp.einsum("vbc,yb,xc->vyx", coverage.astype(jnp.float32), row_onehot, col_onehot)
    mine = lax.dynamic_index_in_dim(grid, lax.axis_index("view"), 0, keepdims=False)
    count = jnp.sum(grid, axis=0)
    for step in range(ITERS):
        predicted = along_x(field, mats[0][0])
        predicted = along_rows(predicted, mats[0][2], half)
        predicted = along_planes(predicted, mats[0][3], half)
        ratio = data / (predicted + 0.05)
        back = along_x(ratio, mats[1][0])
        back = along_rows(back, mats[1][2], half)
        back = along_planes(back, mats[1][3], half)
        term = mine[None] * back
        total = lax.psum(term, "view")
        field = field * total / count[None]
    return field


def solution(mesh):
    placed = (
        P("gz", "xy", None),
        P("view", "gz", "xy", None),
        P("view", None),
        P("view", None, None),
        P(),
    )
    return jax.shard_map(
        on_device, mesh=mesh, in_specs=placed, out_specs=P("gz", "xy", None), check_vma=False
    )
```

```python
import functools

import jax
import jax.numpy as jnp
from jax import lax
from jax.experimental import pallas as pl
from jax.experimental.pallas import tpu as pltpu
from jax.sharding import PartitionSpec as P

BLOCK = 128
ITERS = 2
MESH = pl.DeviceIdType.MESH
F32 = jnp.float32
BF16 = jnp.bfloat16


def split(value):
    high = value.astype(BF16)
    return high, (value - high.astype(F32)).astype(BF16)


def dot(a, b):
    return jnp.dot(a, b, preferred_element_type=F32)


def band(kern, axis, forms):
    marks = []
    for rows, cols, sign, base in forms:
        row = lax.broadcasted_iota(jnp.int32, (rows, cols), 0)
        col = lax.broadcasted_iota(jnp.int32, (rows, cols), 1)
        marks.append(base + sign * (row - col))

    def add_tap(tap, carry):
        total, mats = carry
        value = kern[0, axis, tap]
        return total + value, tuple(
            mat + jnp.where(mark == tap, value, 0.0) for mat, mark in zip(mats, marks)
        )

    zeros = tuple(jnp.zeros(mark.shape, F32) for mark in marks)
    total, mats = lax.fori_loop(0, kern.shape[2], add_tap, (jnp.float32(0.0), zeros))
    return [mat / total for mat in mats]


def kernel(
    strips, cov, shifts, kern, est, views, out,
    fext, bext, vext, data, mid, back, mast, own, term, slots, fin,
    rmat, xfor, xback, zmat, send, recv, local,
):
    slab, strip, width = est.shape
    half = strip // 2
    planes = 2 * slab
    taps = kern.shape[2]
    reach = (taps - 1) // 2
    quarter = planes // 4
    group = 8
    v, s, g = lax.axis_index("view"), lax.axis_index("xy"), lax.axis_index("gz")
    va, vb = lax.div(v, 2), lax.rem(v, 2)
    q = 2 * s + g
    has_prev, has_next = q > 0, q < 2 * strips - 1

    def other_view(k):
        return lax.rem(va + k // 2, 2) * 2 + lax.rem(vb + k % 2, 2)

    sibling = (v, s, 1 - g)
    before = (v, lax.rem(s - 1 + g + strips, strips), 1 - g)
    after = (v, lax.rem(s + g, strips), 1 - g)
    strip_before = lax.rem(s - 1 + strips, strips)
    strip_after = lax.rem(s + 1, strips)

    barrier = pltpu.get_barrier_semaphore()

    def greet(device):
        pl.semaphore_signal(barrier, inc=1, device_id=device, device_id_type=MESH)

    greet(sibling)
    for k in range(1, 4):
        greet((other_view(k), s, g))
        greet((other_view(k), s, 1 - g))

    @pl.when(s > 0)
    def _():
        greet((v, strip_before, 0))
        greet((v, strip_before, 1))

    @pl.when(s < strips - 1)
    def _():
        greet((v, strip_after, 0))
        greet((v, strip_after, 1))

    def remote(src, dst, send_id, recv_id, device):
        return pltpu.make_async_remote_copy(
            src_ref=src, dst_ref=dst, send_sem=send.at[send_id], recv_sem=recv.at[recv_id],
            device_id=device, device_id_type=MESH,
        )

    mine = pl.ds(pl.multiple_of(slab * g, slab), slab)
    lay = pl.multiple_of(half - half * g, half)
    first = fext.at[0]

    def lay_plane(i, carry):
        first[slab * g + i, pl.ds(lay, strip), :] = est[i].astype(BF16)
        vext[slab * g + i, pl.ds(lay, strip), :] = views[0, i]
        return carry

    lax.fori_loop(0, slab, lay_plane, 0)

    @pl.when(q == 0)
    def _():
        vext[:, 0:half, :] = jnp.zeros((planes, half, width), BF16)
        for n in range(ITERS):
            fext[n, :, 0:half, :] = jnp.zeros((planes, half, width), BF16)
            bext[n, :, 0:half, :] = jnp.zeros((planes, half, width), BF16)

    @pl.when(q == 2 * strips - 1)
    def _():
        vext[:, 2 * half :, :] = jnp.zeros((planes, half, width), BF16)
        for n in range(ITERS):
            fext[n, :, 2 * half :, :] = jnp.zeros((planes, half, width), BF16)
            bext[n, :, 2 * half :, :] = jnp.zeros((planes, half, width), BF16)

    pl.semaphore_wait(
        barrier, 7 + 2 * (s > 0).astype(jnp.int32) + 2 * (s < strips - 1).astype(jnp.int32)
    )

    def spread(ext, base):
        src_rows = lay
        across = remote(
            ext.at[mine, pl.ds(lay, strip), :],
            ext.at[mine, pl.ds(pl.multiple_of(half * g, half), strip), :],
            base, base, sibling,
        )
        down = remote(
            ext.at[mine, pl.ds(src_rows, half), :], ext.at[mine, 2 * half : 3 * half, :],
            base + 1, base + 1 + g, (v, strip_before, 1),
        )
        up = remote(
            ext.at[mine, pl.ds(pl.multiple_of(src_rows + half, half), half), :],
            ext.at[mine, 0:half, :],
            base + 2, base + 1 + g, (v, strip_after, 0),
        )
        return across, down, up

    def spread_start(copies):
        across, down, up = copies

        @pl.when(s > 0)
        def _():
            down.start()

        @pl.when(s < strips - 1)
        def _():
            up.start()

        across.start()

    def spread_arrive(ext, base):
        theirs = pl.ds(pl.multiple_of(slab * (1 - g), slab), slab)
        remote(
            ext.at[mine, pl.ds(lay, strip), :], ext.at[theirs, pl.ds(lay, strip), :],
            base, base, sibling,
        ).wait_recv()
        for c in range(2):
            part = pl.ds(c * slab, slab)

            @pl.when(jnp.logical_and(g == 0, s > 0))
            def _():
                remote(
                    ext.at[part, half : 2 * half, :], ext.at[part, 0:half, :],
                    base, base + 1 + c, sibling,
                ).wait_recv()

            @pl.when(jnp.logical_and(g == 1, s < strips - 1))
            def _():
                remote(
                    ext.at[part, half : 2 * half, :], ext.at[part, 2 * half : 3 * half, :],
                    base, base + 1 + c, sibling,
                ).wait_recv()

    def spread_sent(copies):
        across, down, up = copies
        across.wait_send()

        @pl.when(s > 0)
        def _():
            down.wait_send()

        @pl.when(s < strips - 1)
        def _():
            up.wait_send()

    est_copies = spread(first, 0)
    spread_start(est_copies)
    view_copies = spread(vext, 3)
    spread_start(view_copies)
    quarter_here = pl.ds(pl.multiple_of(quarter * vb, quarter), quarter)
    mast_copy = remote(
        est.at[quarter_here, pl.ds(pl.multiple_of(half * (1 - g), half), half), :],
        mast, 6, 6, sibling,
    )

    @pl.when(g == va)
    def _():
        mast_copy.start()
        mast[...] = est[quarter_here, pl.ds(pl.multiple_of(half * g, half), half), :]

    x_forward, = band(kern, 2, [(width, width, 1, reach)])
    x_backward, = band(kern, 2, [(width, width, -1, reach)])
    high, low = split(x_forward)
    xfor[:, :width] = high
    xfor[:, width:] = low
    high, low = split(x_backward)
    xback[:width, :width] = high
    xback[:width, width:] = low
    xback[width:, :width] = high
    xback[width:, width:] = jnp.zeros((width, width), BF16)
    z_mats = band(kern, 0, [(planes, planes, -1, reach), (planes, planes, 1, reach)])
    r_mats = band(
        kern, 1, [(half, 3 * half, -1, reach - half), (half, 3 * half, 1, reach + half)]
    )
    for way in range(2):
        high, low = split(z_mats[way])
        zmat[way, :planes, :] = high
        zmat[way, planes:, :] = low
        high, low = split(r_mats[way])
        rmat[way, :half, :] = high
        rmat[way, half:, :] = low

    def halo(ext, base, k):
        part = pl.ds(pl.multiple_of(quarter * other_view(k), quarter), quarter)
        src = ext.at[part, half : 2 * half, :]
        return (
            remote(src, ext.at[part, 2 * half : 3 * half, :], base + 2 * k, base + 2 * k, before),
            remote(src, ext.at[part, 0:half, :], base + 2 * k + 1, base + 2 * k + 1, after),
        )

    def halo_start(copies):
        down, up = copies

        @pl.when(has_prev)
        def _():
            down.start()

        @pl.when(has_next)
        def _():
            up.start()

    def halo_arrive(copies):
        down, up = copies

        @pl.when(has_next)
        def _():
            down.wait_recv()

        @pl.when(has_prev)
        def _():
            up.wait_recv()

    def halo_sent(copies):
        down, up = copies

        @pl.when(has_prev)
        def _():
            down.wait_send()

        @pl.when(has_next)
        def _():
            up.wait_send()

    def along_rows(ext, way, plane, load=None):
        load = load or (lambda i: ext[plane + i])
        mat = rmat[way]
        parts = []
        for i in range(0, group, 2):
            both = dot(mat, jnp.concatenate([load(i), load(i + 1)], axis=1))
            both = both[:half] + both[half:]
            parts += [both[:, :width], both[:, width:]]
        return jnp.concatenate(parts, axis=0)

    def forward(ext, plane):
        both = dot(along_rows(ext, 0, plane).astype(BF16), xfor[...])
        mid[pl.ds(pl.multiple_of(plane * half, group * half), group * half), :] = (
            both[:, :width] + both[:, width:]
        )

    def backward(ext, plane):
        high, low = split(along_rows(ext, 1, plane))
        both = dot(jnp.concatenate([high, low], axis=1), xback[...])
        return both[:, :width] + both[:, width:]

    def loop(steps, body):
        def step(i, carry):
            body(i)
            return carry

        lax.fori_loop(0, steps, step, 0)

    block = lax.div(q * half, BLOCK)
    weight = cov[v, block, 0].astype(F32)
    count = jnp.float32(0.0)
    for n in range(4):
        count = count + cov[n, block, 0].astype(F32)

    spread_arrive(first, 0)
    loop(planes // group, lambda i: forward(first, group * i))

    spread_arrive(vext, 3)
    row = lax.broadcasted_iota(jnp.int32, (half, 3 * half), 0)
    col = lax.broadcasted_iota(jnp.int32, (half, 3 * half), 1)
    pick_rows = (col == row + half + shifts[0, 1]).astype(F32).astype(BF16)
    row = lax.broadcasted_iota(jnp.int32, (width, width), 0)
    col = lax.broadcasted_iota(jnp.int32, (width, width), 1)
    pick_x = (row == col + shifts[0, 2]).astype(F32).astype(BF16)

    def window(i):
        parts = []
        for j in range(0, group, 2):
            pair, masks = [], []
            for n in range(2):
                plane = group * i + j + n + shifts[0, 0]
                inside = jnp.logical_and(plane >= 0, plane < planes)
                masks.append(inside.astype(jnp.int32).astype(F32))
                pair.append(vext[jnp.clip(plane, 0, planes - 1)])
            both = dot(pick_rows, jnp.concatenate(pair, axis=1))
            parts += [both[:, :width] * masks[0], both[:, width:] * masks[1]]
        moved = dot(jnp.concatenate(parts, axis=0).astype(BF16), pick_x)
        data[pl.ds(pl.multiple_of(group * half * i, group * half), group * half), :] = moved

    loop(planes // group, window)

    def column(ref, y):
        return jnp.concatenate(
            [ref[pl.ds(y, planes, stride=half), :], ref[pl.ds(y + 1, planes, stride=half), :]],
            axis=1,
        )

    def along_planes(i):
        for j in range(0, 4, 2):
            y = 4 * i + j
            both = dot(zmat[0], column(mid, y).astype(BF16))
            predicted = both[:planes] + both[planes:]
            ratio = column(data, y) / (predicted + 0.05)
            both = dot(zmat[1], ratio.astype(BF16))
            both = both[:planes] + both[planes:]
            back[pl.ds(y, planes, stride=half), :] = both[:, :width]
            back[pl.ds(y + 1, planes, stride=half), :] = both[:, width:]

    quarter_rows = quarter * half
    halos, terms, gathers = [], [], []
    for step in range(ITERS):
        loop(half // 4, along_planes)
        ext = bext.at[step]
        copies = {}
        for k in (3, 1, 2, 0):
            start = quarter * other_view(k)

            def lay_back(i):
                at = pl.multiple_of((start + i) * half, half)
                ext[start + i, half : 2 * half, :] = back[pl.ds(at, half), :].astype(BF16)

            loop(quarter, lay_back)
            copies[k] = halo(ext, 7 + 16 * step, k)
            halo_start(copies[k])
        for k in (3, 1, 2, 0):
            halo_arrive(copies[k])
            start = quarter * other_view(k)
            dest = own if k == 0 else term.at[step, k - 1]

            def correct(i):
                at = pl.multiple_of(group * half * i, group * half)
                dest[pl.ds(at, group * half), :] = weight * backward(ext, start + group * i)

            loop(quarter // group, correct)
            if k:
                sent = remote(
                    dest, slots.at[step, k - 1], 31 + 3 * step + k - 1, 31 + 3 * step + k - 1,
                    (other_view(k), s, g),
                )
                sent.start()
                terms.append(sent)
        halos += list(copies.values())
        if step == 0:

            @pl.when(g != va)
            def _():
                mast_copy.wait_recv()

        for sent in terms[-3:]:
            sent.wait_recv()
        last = step == ITERS - 1
        here = quarter * v

        def update(i):
            rows = pl.ds(pl.multiple_of(i * half, half), half)
            total = own[rows, :]
            for k in range(3):
                total = total + slots[step, k, rows, :]
            field = mast[i] * total / count
            if last:
                fin[i] = field
            else:
                mast[i] = field
                fext[step + 1, here + i, half : 2 * half, :] = field.astype(BF16)

        loop(quarter, update)
        if last:
            break
        ext = fext.at[step + 1]
        part = ext.at[pl.ds(pl.multiple_of(here, quarter), quarter), half : 2 * half, :]
        news = []
        for k in (3, 1, 2):
            sent = remote(part, part, 37 + k - 1, 37 + k - 1, (other_view(k), s, g))
            sent.start()
            news.append((k, sent))
        copies = [halo(ext, 47, k) for k in range(4)]
        halo_start(copies[0])
        for k in (1, 2, 3):
            theirs = ext.at[
                pl.ds(pl.multiple_of(quarter * other_view(k), quarter), quarter),
                half : 2 * half, :,
            ]
            remote(theirs, theirs, 37 + k - 1, 37 + k - 1, sibling).wait_recv()
            halo_start(copies[k])
        for k in range(4):
            halo_arrive(copies[k])
            start = quarter * other_view(k)
            loop(quarter // group, lambda i: forward(ext, start + group * i))
        halos += copies
        gathers += [sent for _, sent in news]

    place = out.at[
        quarter_here, pl.ds(pl.multiple_of(half * g, half), half), :
    ]
    arrive = 40 + 2 * vb + g
    results = [remote(fin, place, 40 + k, arrive, (other_view(k), s, va)) for k in range(4)]
    keep = pltpu.make_async_copy(fin, place, local.at[0])
    for k in (3, 1, 2):
        results[k].start()

    @pl.when(g == va)
    def _():
        keep.start()

    @pl.when(g != va)
    def _():
        results[0].start()

    for a in range(2):
        for b in range(2):
            spot = out.at[quarter * a : quarter * (a + 1), half * b : half * (b + 1), :]

            @pl.when(jnp.logical_or(v != 2 * g + a, g != b))
            def _():
                remote(fin, spot, 40, 40 + 2 * a + b, sibling).wait_recv()

    @pl.when(g == va)
    def _():
        keep.wait()
        mast_copy.wait_send()

    @pl.when(g != va)
    def _():
        results[0].wait_send()

    for k in (1, 2, 3):
        results[k].wait_send()
    spread_sent(est_copies)
    spread_sent(view_copies)
    for copies in halos:
        halo_sent(copies)
    for sent in terms + gathers:
        sent.wait_send()


def on_device(strips, estimate, views, shifts, kernels, coverage):
    slab, strip, width = estimate.shape
    half, planes = strip // 2, 2 * slab
    quarter = planes // 4
    vmem = pl.BlockSpec(memory_space=pltpu.VMEM)
    smem = pl.BlockSpec(memory_space=pltpu.SMEM)
    rows = planes * half
    scratch = [
        pltpu.VMEM((ITERS, planes, 3 * half, width), BF16),
        pltpu.VMEM((ITERS, planes, 3 * half, width), BF16),
        pltpu.VMEM((planes, 3 * half, width), BF16),
        pltpu.VMEM((rows, width), F32),
        pltpu.VMEM((rows, width), F32),
        pltpu.VMEM((rows, width), F32),
        pltpu.VMEM((quarter, half, width), F32),
        pltpu.VMEM((quarter * half, width), F32),
        pltpu.VMEM((ITERS, 3, quarter * half, width), F32),
        pltpu.VMEM((ITERS, 3, quarter * half, width), F32),
        pltpu.VMEM((quarter, half, width), F32),
        pltpu.VMEM((2, 2 * half, 3 * half), BF16),
        pltpu.VMEM((width, 2 * width), BF16),
        pltpu.VMEM((2 * width, 2 * width), BF16),
        pltpu.VMEM((2, 2 * planes, planes), BF16),
        pltpu.SemaphoreType.DMA((56,)),
        pltpu.SemaphoreType.DMA((56,)),
        pltpu.SemaphoreType.DMA((1,)),
    ]
    return pl.pallas_call(
        functools.partial(kernel, strips),
        out_shape=jax.ShapeDtypeStruct(estimate.shape, F32),
        in_specs=[smem, smem, smem, vmem, vmem],
        out_specs=pl.BlockSpec(memory_space=pl.ANY),
        scratch_shapes=scratch,
        compiler_params=pltpu.CompilerParams(
            collective_id=0, has_side_effects=True, vmem_limit_bytes=40 * 1024 * 1024
        ),
        cost_estimate=pl.CostEstimate(
            flops=12 * 2 * rows * width * 100, bytes_accessed=8 * rows * width, transcendentals=0
        ),
    )(coverage, shifts, kernels, estimate, views)


def solution(mesh):
    placed = (
        P("gz", "xy", None),
        P("view", "gz", "xy", None),
        P("view", None),
        P("view", None, None),
        P(),
    )
    return jax.shard_map(
        functools.partial(on_device, mesh.shape["xy"]),
        mesh=mesh, in_specs=placed, out_specs=P("gz", "xy", None), check_vma=False,
    )
```

```python
import functools

import jax
import jax.numpy as jnp
from jax import lax
from jax.experimental import pallas as pl
from jax.experimental.pallas import tpu as pltpu
from jax.sharding import PartitionSpec as P

BLOCK = 128
ITERS = 2
MESH = pl.DeviceIdType.MESH
F32 = jnp.float32
BF16 = jnp.bfloat16


def split(value):
    high = value.astype(BF16)
    return high, (value - high.astype(F32)).astype(BF16)


def dot(a, b):
    return jnp.dot(a, b, preferred_element_type=F32)


def band(kern, axis, forms):
    marks = []
    for rows, cols, sign, base in forms:
        row = lax.broadcasted_iota(jnp.int32, (rows, cols), 0)
        col = lax.broadcasted_iota(jnp.int32, (rows, cols), 1)
        marks.append(base + sign * (row - col))

    def add_tap(tap, carry):
        total, mats = carry
        value = kern[0, axis, tap]
        return total + value, tuple(
            mat + jnp.where(mark == tap, value, 0.0) for mat, mark in zip(mats, marks)
        )

    zeros = tuple(jnp.zeros(mark.shape, F32) for mark in marks)
    total, mats = lax.fori_loop(0, kern.shape[2], add_tap, (jnp.float32(0.0), zeros))
    return [mat / total for mat in mats]


def kernel(
    strips, cov, shifts, kern, given, views, out,
    est, fext, bext, vext, data, mid, back, mast, own, term, slots, fin,
    rmat, xfor, xback, zmat, send, recv, local,
):
    slab, strip, width = est.shape
    half = strip // 2
    planes = 2 * slab
    taps = kern.shape[2]
    reach = (taps - 1) // 2
    quarter = planes // 4
    group = 8
    v, s, g = lax.axis_index("view"), lax.axis_index("xy"), lax.axis_index("gz")
    va, vb = lax.div(v, 2), lax.rem(v, 2)
    q = 2 * s + g
    has_prev, has_next = q > 0, q < 2 * strips - 1

    def other_view(k):
        return lax.rem(va + k // 2, 2) * 2 + lax.rem(vb + k % 2, 2)

    fetch = pltpu.make_async_copy(given, est, local.at[0])
    fetch.start()
    sibling = (v, s, 1 - g)
    before = (v, lax.rem(s - 1 + g + strips, strips), 1 - g)
    after = (v, lax.rem(s + g, strips), 1 - g)
    strip_before = lax.rem(s - 1 + strips, strips)
    strip_after = lax.rem(s + 1, strips)

    barrier = pltpu.get_barrier_semaphore()

    def greet(device):
        pl.semaphore_signal(barrier, inc=1, device_id=device, device_id_type=MESH)

    greet(sibling)
    for k in range(1, 4):
        greet((other_view(k), s, g))
        greet((other_view(k), s, 1 - g))

    @pl.when(s > 0)
    def _():
        greet((v, strip_before, 0))
        greet((v, strip_before, 1))

    @pl.when(s < strips - 1)
    def _():
        greet((v, strip_after, 0))
        greet((v, strip_after, 1))

    def remote(src, dst, send_id, recv_id, device):
        return pltpu.make_async_remote_copy(
            src_ref=src, dst_ref=dst, send_sem=send.at[send_id], recv_sem=recv.at[recv_id],
            device_id=device, device_id_type=MESH,
        )

    mine = pl.ds(pl.multiple_of(slab * g, slab), slab)
    lay = pl.multiple_of(half - half * g, half)
    first = fext.at[0]

    lay_views = pltpu.make_async_copy(
        views.at[0], vext.at[mine, pl.ds(lay, strip), :], local.at[1]
    )
    lay_views.start()

    @pl.when(q == 0)
    def _():
        vext[:, 0:half, :] = jnp.zeros((planes, half, width), BF16)
        for n in range(ITERS):
            fext[n, :, 0:half, :] = jnp.zeros((planes, half, width), BF16)
            bext[n, :, 0:half, :] = jnp.zeros((planes, half, width), BF16)

    @pl.when(q == 2 * strips - 1)
    def _():
        vext[:, 2 * half :, :] = jnp.zeros((planes, half, width), BF16)
        for n in range(ITERS):
            fext[n, :, 2 * half :, :] = jnp.zeros((planes, half, width), BF16)
            bext[n, :, 2 * half :, :] = jnp.zeros((planes, half, width), BF16)

    fetch.wait()
    for i in range(0, slab, group):
        first[pl.ds(slab * g + i, group), pl.ds(lay, strip), :] = est[i : i + group].astype(BF16)

    pl.semaphore_wait(
        barrier, 7 + 2 * (s > 0).astype(jnp.int32) + 2 * (s < strips - 1).astype(jnp.int32)
    )

    def spread(ext, base, block):
        across = remote(
            block,
            ext.at[mine, pl.ds(pl.multiple_of(half * g, half), strip), :],
            base, base, sibling,
        )
        down = remote(
            block.at[:, 0:half, :], ext.at[mine, 2 * half : 3 * half, :],
            base + 1, base + 1 + g, (v, strip_before, 1),
        )
        up = remote(
            block.at[:, half:strip, :], ext.at[mine, 0:half, :],
            base + 2, base + 1 + g, (v, strip_after, 0),
        )
        return across, down, up

    def spread_start(copies):
        across, down, up = copies

        @pl.when(s > 0)
        def _():
            down.start()

        @pl.when(s < strips - 1)
        def _():
            up.start()

        across.start()

    def spread_arrive(ext, base):
        theirs = pl.ds(pl.multiple_of(slab * (1 - g), slab), slab)
        remote(
            ext.at[mine, pl.ds(lay, strip), :], ext.at[theirs, pl.ds(lay, strip), :],
            base, base, sibling,
        ).wait_recv()
        for c in range(2):
            part = pl.ds(c * slab, slab)

            @pl.when(jnp.logical_and(g == 0, s > 0))
            def _():
                remote(
                    ext.at[part, half : 2 * half, :], ext.at[part, 0:half, :],
                    base, base + 1 + c, sibling,
                ).wait_recv()

            @pl.when(jnp.logical_and(g == 1, s < strips - 1))
            def _():
                remote(
                    ext.at[part, half : 2 * half, :], ext.at[part, 2 * half : 3 * half, :],
                    base, base + 1 + c, sibling,
                ).wait_recv()

    def spread_sent(copies):
        across, down, up = copies
        across.wait_send()

        @pl.when(s > 0)
        def _():
            down.wait_send()

        @pl.when(s < strips - 1)
        def _():
            up.wait_send()

    est_copies = spread(first, 0, first.at[mine, pl.ds(lay, strip), :])
    spread_start(est_copies)
    view_copies = spread(vext, 3, views.at[0])
    quarter_here = pl.ds(pl.multiple_of(quarter * vb, quarter), quarter)
    mast_copy = remote(
        est.at[quarter_here, pl.ds(pl.multiple_of(half * (1 - g), half), half), :],
        mast, 6, 6, sibling,
    )

    @pl.when(g == va)
    def _():
        mast_copy.start()
        mast[...] = est[quarter_here, pl.ds(pl.multiple_of(half * g, half), half), :]

    x_forward, = band(kern, 2, [(width, width, 1, reach)])
    x_backward, = band(kern, 2, [(width, width, -1, reach)])
    high, low = split(x_forward)
    xfor[:, :width] = high
    xfor[:, width:] = low
    high, low = split(x_backward)
    xback[:width, :width] = high
    xback[:width, width:] = low
    xback[width:, :width] = high
    xback[width:, width:] = jnp.zeros((width, width), BF16)
    z_mats = band(kern, 0, [(planes, planes, -1, reach), (planes, planes, 1, reach)])
    r_mats = band(
        kern, 1, [(half, 3 * half, -1, reach - half), (half, 3 * half, 1, reach + half)]
    )
    for way in range(2):
        high, low = split(z_mats[way])
        zmat[way, :planes, :] = high
        zmat[way, planes:, :] = low
        high, low = split(r_mats[way])
        rmat[way, :half, :] = high
        rmat[way, half:, :] = low

    def halo(ext, base, k):
        part = pl.ds(pl.multiple_of(quarter * other_view(k), quarter), quarter)
        src = ext.at[part, half : 2 * half, :]
        return (
            remote(src, ext.at[part, 2 * half : 3 * half, :], base + 2 * k, base + 2 * k, before),
            remote(src, ext.at[part, 0:half, :], base + 2 * k + 1, base + 2 * k + 1, after),
        )

    def halo_start(copies):
        down, up = copies

        @pl.when(has_prev)
        def _():
            down.start()

        @pl.when(has_next)
        def _():
            up.start()

    def halo_arrive(copies):
        down, up = copies

        @pl.when(has_next)
        def _():
            down.wait_recv()

        @pl.when(has_prev)
        def _():
            up.wait_recv()

    def halo_sent(copies):
        down, up = copies

        @pl.when(has_prev)
        def _():
            down.wait_send()

        @pl.when(has_next)
        def _():
            up.wait_send()

    def along_rows(ext, way, plane, load=None):
        load = load or (lambda i: ext[plane + i])
        mat = rmat[way]
        parts = []
        for i in range(0, group, 2):
            both = dot(mat, jnp.concatenate([load(i), load(i + 1)], axis=1))
            both = both[:half] + both[half:]
            parts += [both[:, :width], both[:, width:]]
        return jnp.concatenate(parts, axis=0)

    def forward(ext, plane):
        both = dot(along_rows(ext, 0, plane).astype(BF16), xfor[...])
        mid[pl.ds(pl.multiple_of(plane * half, group * half), group * half), :] = (
            both[:, :width] + both[:, width:]
        )

    def backward(ext, plane):
        high, low = split(along_rows(ext, 1, plane))
        both = dot(jnp.concatenate([high, low], axis=1), xback[...])
        return both[:, :width] + both[:, width:]

    def loop(steps, body, wide=1):
        def step(i, carry):
            for n in range(wide):
                body(wide * i + n)
            return carry

        lax.fori_loop(0, steps // wide, step, 0)

    block = lax.div(q * half, BLOCK)
    weight = cov[v, block, 0].astype(F32)
    count = jnp.float32(0.0)
    for n in range(4):
        count = count + cov[n, block, 0].astype(F32)

    spread_arrive(first, 0)
    spread_start(view_copies)
    loop(planes // group, lambda i: forward(first, group * i), 2)

    lay_views.wait()
    spread_arrive(vext, 3)
    row = lax.broadcasted_iota(jnp.int32, (half, 3 * half), 0)
    col = lax.broadcasted_iota(jnp.int32, (half, 3 * half), 1)
    pick_rows = (col == row + half + shifts[0, 1]).astype(F32).astype(BF16)
    row = lax.broadcasted_iota(jnp.int32, (width, width), 0)
    col = lax.broadcasted_iota(jnp.int32, (width, width), 1)
    pick_x = (row == col + shifts[0, 2]).astype(F32).astype(BF16)

    def window(i):
        parts = []
        for j in range(0, group, 2):
            pair, masks = [], []
            for n in range(2):
                plane = group * i + j + n + shifts[0, 0]
                inside = jnp.logical_and(plane >= 0, plane < planes)
                masks.append(inside.astype(jnp.int32).astype(F32))
                pair.append(vext[jnp.clip(plane, 0, planes - 1)])
            both = dot(pick_rows, jnp.concatenate(pair, axis=1))
            parts += [both[:, :width] * masks[0], both[:, width:] * masks[1]]
        moved = dot(jnp.concatenate(parts, axis=0).astype(BF16), pick_x)
        data[pl.ds(pl.multiple_of(group * half * i, group * half), group * half), :] = moved

    loop(planes // group, window, 2)

    def column(ref, y):
        return jnp.concatenate(
            [ref[pl.ds(y, planes, stride=half), :], ref[pl.ds(y + 1, planes, stride=half), :]],
            axis=1,
        )

    def along_planes(i):
        for j in range(0, 4, 2):
            y = 4 * i + j
            both = dot(zmat[0], column(mid, y).astype(BF16))
            predicted = both[:planes] + both[planes:]
            ratio = column(data, y) / (predicted + 0.05)
            both = dot(zmat[1], ratio.astype(BF16))
            both = both[:planes] + both[planes:]
            back[pl.ds(y, planes, stride=half), :] = both[:, :width]
            back[pl.ds(y + 1, planes, stride=half), :] = both[:, width:]

    quarter_rows = quarter * half
    halos, terms, gathers = [], [], []
    for step in range(ITERS):
        loop(half // 4, along_planes, 2)
        ext = bext.at[step]
        copies = {}
        for k in (3, 1, 2, 0):
            start = quarter * other_view(k)

            at = pl.multiple_of(start * half, quarter * half)
            ext[pl.ds(start, quarter), half : 2 * half, :] = (
                back[pl.ds(at, quarter * half), :].reshape(quarter, half, width).astype(BF16)
            )
            copies[k] = halo(ext, 7 + 16 * step, k)
            halo_start(copies[k])
        for k in (3, 1, 2, 0):
            halo_arrive(copies[k])
            start = quarter * other_view(k)
            dest = own if k == 0 else term.at[step, k - 1]

            def correct(i):
                at = pl.multiple_of(group * half * i, group * half)
                dest[pl.ds(at, group * half), :] = weight * backward(ext, start + group * i)

            loop(quarter // group, correct, 2)
            if k:
                sent = remote(
                    dest, slots.at[step, k - 1], 31 + 3 * step + k - 1, 31 + 3 * step + k - 1,
                    (other_view(k), s, g),
                )
                sent.start()
                terms.append(sent)
        halos += list(copies.values())
        if step == 0:

            @pl.when(g != va)
            def _():
                mast_copy.wait_recv()

        for sent in terms[-3:]:
            sent.wait_recv()
        last = step == ITERS - 1
        here = quarter * v

        def update(i):
            rows = pl.ds(pl.multiple_of(i * group * half, group * half), group * half)
            total = own[rows, :]
            for k in range(3):
                total = total + slots[step, k, rows, :]
            at = pl.ds(pl.multiple_of(i * group, group), group)
            field = mast[at] * total.reshape(group, half, width) / count
            if last:
                fin[at] = field
            else:
                mast[at] = field
                fext[step + 1, pl.ds(here + i * group, group), half : 2 * half, :] = field.astype(
                    BF16
                )

        loop(quarter // group, update)
        if last:
            break
        ext = fext.at[step + 1]
        part = ext.at[pl.ds(pl.multiple_of(here, quarter), quarter), half : 2 * half, :]
        news = []
        for k in (3, 1, 2):
            sent = remote(part, part, 37 + k - 1, 37 + k - 1, (other_view(k), s, g))
            sent.start()
            news.append((k, sent))
        copies = [halo(ext, 47, k) for k in range(4)]
        halo_start(copies[0])
        for k in (1, 2, 3):
            theirs = ext.at[
                pl.ds(pl.multiple_of(quarter * other_view(k), quarter), quarter),
                half : 2 * half, :,
            ]
            remote(theirs, theirs, 37 + k - 1, 37 + k - 1, sibling).wait_recv()
            halo_start(copies[k])
        for k in range(4):
            halo_arrive(copies[k])
            start = quarter * other_view(k)
            loop(quarter // group, lambda i: forward(ext, start + group * i), 2)
        halos += copies
        gathers += [sent for _, sent in news]

    place = out.at[
        quarter_here, pl.ds(pl.multiple_of(half * g, half), half), :
    ]
    arrive = 40 + 2 * vb + g
    results = [remote(fin, place, 40 + k, arrive, (other_view(k), s, va)) for k in range(4)]
    keep = pltpu.make_async_copy(fin, place, local.at[0])
    for k in (3, 1, 2):
        results[k].start()

    @pl.when(g == va)
    def _():
        keep.start()

    @pl.when(g != va)
    def _():
        results[0].start()

    for a in range(2):
        for b in range(2):
            spot = out.at[quarter * a : quarter * (a + 1), half * b : half * (b + 1), :]

            @pl.when(jnp.logical_or(v != 2 * g + a, g != b))
            def _():
                remote(fin, spot, 40, 40 + 2 * a + b, sibling).wait_recv()

    @pl.when(g == va)
    def _():
        keep.wait()
        mast_copy.wait_send()

    @pl.when(g != va)
    def _():
        results[0].wait_send()

    for k in (1, 2, 3):
        results[k].wait_send()
    spread_sent(est_copies)
    spread_sent(view_copies)
    for copies in halos:
        halo_sent(copies)
    for sent in terms + gathers:
        sent.wait_send()


def on_device(strips, estimate, views, shifts, kernels, coverage):
    slab, strip, width = estimate.shape
    half, planes = strip // 2, 2 * slab
    quarter = planes // 4
    hbm = pl.BlockSpec(memory_space=pl.ANY)
    smem = pl.BlockSpec(memory_space=pltpu.SMEM)
    rows = planes * half
    scratch = [
        pltpu.VMEM(estimate.shape, F32),
        pltpu.VMEM((ITERS, planes, 3 * half, width), BF16),
        pltpu.VMEM((ITERS, planes, 3 * half, width), BF16),
        pltpu.VMEM((planes, 3 * half, width), BF16),
        pltpu.VMEM((rows, width), F32),
        pltpu.VMEM((rows, width), F32),
        pltpu.VMEM((rows, width), F32),
        pltpu.VMEM((quarter, half, width), F32),
        pltpu.VMEM((quarter * half, width), F32),
        pltpu.VMEM((ITERS, 3, quarter * half, width), F32),
        pltpu.VMEM((ITERS, 3, quarter * half, width), F32),
        pltpu.VMEM((quarter, half, width), F32),
        pltpu.VMEM((2, 2 * half, 3 * half), BF16),
        pltpu.VMEM((width, 2 * width), BF16),
        pltpu.VMEM((2 * width, 2 * width), BF16),
        pltpu.VMEM((2, 2 * planes, planes), BF16),
        pltpu.SemaphoreType.DMA((56,)),
        pltpu.SemaphoreType.DMA((56,)),
        pltpu.SemaphoreType.DMA((2,)),
    ]
    return pl.pallas_call(
        functools.partial(kernel, strips),
        out_shape=jax.ShapeDtypeStruct(estimate.shape, F32),
        in_specs=[smem, smem, smem, hbm, hbm],
        out_specs=hbm,
        scratch_shapes=scratch,
        compiler_params=pltpu.CompilerParams(
            collective_id=0, has_side_effects=True, vmem_limit_bytes=40 * 1024 * 1024
        ),
        cost_estimate=pl.CostEstimate(
            flops=12 * 2 * rows * width * 100, bytes_accessed=8 * rows * width, transcendentals=0
        ),
    )(coverage, shifts, kernels, estimate, views)


def solution(mesh):
    placed = (
        P("gz", "xy", None),
        P("view", "gz", "xy", None),
        P("view", None),
        P("view", None, None),
        P(),
    )
    return jax.shard_map(
        functools.partial(on_device, mesh.shape["xy"]),
        mesh=mesh, in_specs=placed, out_specs=P("gz", "xy", None), check_vma=False,
    )
```

```python
import functools

import jax
import jax.numpy as jnp
from jax import lax
from jax.experimental import pallas as pl
from jax.experimental.pallas import tpu as pltpu
from jax.sharding import PartitionSpec as P

BLOCK = 128
ITERS = 2
MESH = pl.DeviceIdType.MESH
F32 = jnp.float32
BF16 = jnp.bfloat16


def split(value):
    high = value.astype(BF16)
    return high, (value - high.astype(F32)).astype(BF16)


def dot(a, b):
    return jnp.dot(a, b, preferred_element_type=F32)


def band(kern, axis, forms):
    marks = []
    for rows, cols, sign, base in forms:
        row = lax.broadcasted_iota(jnp.int32, (rows, cols), 0)
        col = lax.broadcasted_iota(jnp.int32, (rows, cols), 1)
        marks.append(base + sign * (row - col))

    def add_tap(tap, carry):
        total, mats = carry
        value = kern[0, axis, tap]
        return total + value, tuple(
            mat + jnp.where(mark == tap, value, 0.0) for mat, mark in zip(mats, marks)
        )

    zeros = tuple(jnp.zeros(mark.shape, F32) for mark in marks)
    total, mats = lax.fori_loop(0, kern.shape[2], add_tap, (jnp.float32(0.0), zeros))
    return [mat / total for mat in mats]


def kernel(
    strips, cov, shifts, kern, given, views, out,
    est, fext, bext, vext, data, mid, back, mast, own, term, slots, relay, fin,
    rmat, xfor, xback, zmat, send, recv, local,
):
    slab, strip, width = est.shape
    half = strip // 2
    planes = 2 * slab
    taps = kern.shape[2]
    reach = (taps - 1) // 2
    quarter = planes // 4
    group = quarter // 2
    v, s, g = lax.axis_index("view"), lax.axis_index("xy"), lax.axis_index("gz")
    va, vb = lax.div(v, 2), lax.rem(v, 2)
    q = 2 * s + g
    has_prev, has_next = q > 0, q < 2 * strips - 1

    def other_view(k):
        return lax.rem(va + k // 2, 2) * 2 + lax.rem(vb + k % 2, 2)

    fetch = pltpu.make_async_copy(given, est, local.at[0])
    fetch.start()
    sibling = (v, s, 1 - g)
    before = (v, lax.rem(s - 1 + g + strips, strips), 1 - g)
    after = (v, lax.rem(s + g, strips), 1 - g)
    strip_before = lax.rem(s - 1 + strips, strips)
    strip_after = lax.rem(s + 1, strips)

    barrier = pltpu.get_barrier_semaphore()

    def greet(device):
        pl.semaphore_signal(barrier, inc=1, device_id=device, device_id_type=MESH)

    greet(sibling)
    for k in range(1, 4):
        greet((other_view(k), s, g))
        greet((other_view(k), s, 1 - g))

    @pl.when(s > 0)
    def _():
        greet((v, strip_before, 0))
        greet((v, strip_before, 1))

    @pl.when(s < strips - 1)
    def _():
        greet((v, strip_after, 0))
        greet((v, strip_after, 1))

    def remote(src, dst, send_id, recv_id, device):
        return pltpu.make_async_remote_copy(
            src_ref=src, dst_ref=dst, send_sem=send.at[send_id], recv_sem=recv.at[recv_id],
            device_id=device, device_id_type=MESH,
        )

    mine = pl.ds(pl.multiple_of(slab * g, slab), slab)
    lay = pl.multiple_of(half - half * g, half)
    first = fext.at[0]

    lay_views = pltpu.make_async_copy(
        views.at[0], vext.at[mine, pl.ds(lay, strip), :], local.at[1]
    )
    lay_views.start()

    @pl.when(q == 0)
    def _():
        vext[:, 0:half, :] = jnp.zeros((planes, half, width), BF16)
        for n in range(ITERS):
            fext[n, :, 0:half, :] = jnp.zeros((planes, half, width), BF16)
            bext[n, :, 0:half, :] = jnp.zeros((planes, half, width), BF16)

    @pl.when(q == 2 * strips - 1)
    def _():
        vext[:, 2 * half :, :] = jnp.zeros((planes, half, width), BF16)
        for n in range(ITERS):
            fext[n, :, 2 * half :, :] = jnp.zeros((planes, half, width), BF16)
            bext[n, :, 2 * half :, :] = jnp.zeros((planes, half, width), BF16)

    fetch.wait()
    for i in range(0, slab, group):
        first[pl.ds(slab * g + i, group), pl.ds(lay, strip), :] = est[i : i + group].astype(BF16)

    pl.semaphore_wait(
        barrier, 7 + 2 * (s > 0).astype(jnp.int32) + 2 * (s < strips - 1).astype(jnp.int32)
    )

    def spread(ext, base, block):
        across = remote(
            block,
            ext.at[mine, pl.ds(pl.multiple_of(half * g, half), strip), :],
            base, base, sibling,
        )
        down, up = [], []
        for j in range(2):
            src = block.at[quarter * j : quarter * (j + 1)]
            part = pl.ds(pl.multiple_of(slab * g + quarter * j, quarter), quarter)
            down.append(
                remote(
                    src.at[:, 0:half, :], ext.at[part, 2 * half : 3 * half, :],
                    base + 1 + j, base + 1 + 2 * g + j, (v, strip_before, 1),
                )
            )
            up.append(
                remote(
                    src.at[:, half:strip, :], ext.at[part, 0:half, :],
                    base + 3 + j, base + 1 + 2 * g + j, (v, strip_after, 0),
                )
            )
        return across, down, up

    def spread_start(copies):
        across, down, up = copies

        @pl.when(s > 0)
        def _():
            for copy in down:
                copy.start()

        @pl.when(s < strips - 1)
        def _():
            for copy in up:
                copy.start()

        across.start()

    def across_arrive(ext, base):
        theirs = pl.ds(pl.multiple_of(slab * (1 - g), slab), slab)
        remote(
            ext.at[mine, pl.ds(lay, strip), :], ext.at[theirs, pl.ds(lay, strip), :],
            base, base, sibling,
        ).wait_recv()

    def spread_arrive(ext, base, c, j):
        part = pl.ds(c * slab + j * quarter, quarter)
        number = base + 1 + 2 * c + j

        @pl.when(jnp.logical_and(g == 0, s > 0))
        def _():
            remote(
                ext.at[part, half : 2 * half, :], ext.at[part, 0:half, :],
                number, number, sibling,
            ).wait_recv()

        @pl.when(jnp.logical_and(g == 1, s < strips - 1))
        def _():
            remote(
                ext.at[part, half : 2 * half, :], ext.at[part, 2 * half : 3 * half, :],
                number, number, sibling,
            ).wait_recv()

    def spread_sent(copies):
        across, down, up = copies
        across.wait_send()

        @pl.when(s > 0)
        def _():
            for copy in down:
                copy.wait_send()

        @pl.when(s < strips - 1)
        def _():
            for copy in up:
                copy.wait_send()

    est_copies = spread(first, 0, first.at[mine, pl.ds(lay, strip), :])
    spread_start(est_copies)
    view_copies = spread(vext, 5, views.at[0])
    quarter_here = pl.ds(pl.multiple_of(quarter * vb, quarter), quarter)
    mast_copy = remote(
        est.at[quarter_here, pl.ds(pl.multiple_of(half * (1 - g), half), half), :],
        mast, 10, 10, sibling,
    )

    @pl.when(g == va)
    def _():
        mast_copy.start()
        mast[...] = est[quarter_here, pl.ds(pl.multiple_of(half * g, half), half), :]

    x_forward, = band(kern, 2, [(width, width, 1, reach)])
    x_backward, = band(kern, 2, [(width, width, -1, reach)])
    high, low = split(x_forward)
    xfor[:, :width] = high
    xfor[:, width:] = low
    high, low = split(x_backward)
    xback[:width, :width] = high
    xback[:width, width:] = low
    xback[width:, :width] = high
    xback[width:, width:] = jnp.zeros((width, width), BF16)
    z_mats = band(kern, 0, [(planes, planes, -1, reach), (planes, planes, 1, reach)])
    r_mats = band(
        kern, 1, [(half, 3 * half, -1, reach - half), (half, 3 * half, 1, reach + half)]
    )
    for way in range(2):
        high, low = split(z_mats[way])
        zmat[way, :planes, :] = high
        zmat[way, planes:, :] = low
        high, low = split(r_mats[way])
        rmat[way, :half, :] = high
        rmat[way, half:, :] = low

    def piece(k, h):
        return pl.ds(pl.multiple_of(quarter * other_view(k) + group * h, group), group)

    def halo(ext, base, k, h):
        part = piece(k, h)
        src = ext.at[part, half : 2 * half, :]
        at = base + 4 * k + 2 * h
        return (
            remote(src, ext.at[part, 2 * half : 3 * half, :], at, at, before),
            remote(src, ext.at[part, 0:half, :], at + 1, at + 1, after),
        )

    def halo_start(copies):
        down, up = copies

        @pl.when(has_prev)
        def _():
            down.start()

        @pl.when(has_next)
        def _():
            up.start()

    def halo_arrive(copies):
        down, up = copies

        @pl.when(has_next)
        def _():
            down.wait_recv()

        @pl.when(has_prev)
        def _():
            up.wait_recv()

    def halo_sent(copies):
        down, up = copies

        @pl.when(has_prev)
        def _():
            down.wait_send()

        @pl.when(has_next)
        def _():
            up.wait_send()

    def along_rows(ext, way, plane):
        mat = rmat[way]
        parts = []
        for i in range(0, group, 2):
            both = dot(mat, jnp.concatenate([ext[plane + i], ext[plane + i + 1]], axis=1))
            both = both[:half] + both[half:]
            parts += [both[:, :width], both[:, width:]]
        return jnp.concatenate(parts, axis=0)

    def forward(ext, plane):
        both = dot(along_rows(ext, 0, plane).astype(BF16), xfor[...])
        mid[pl.ds(pl.multiple_of(plane * half, group * half), group * half), :] = (
            both[:, :width] + both[:, width:]
        )

    def backward(ext, plane):
        high, low = split(along_rows(ext, 1, plane))
        both = dot(jnp.concatenate([high, low], axis=1), xback[...])
        return both[:, :width] + both[:, width:]

    def loop(steps, body, wide=1):
        def step(i, carry):
            for n in range(wide):
                body(wide * i + n)
            return carry

        lax.fori_loop(0, steps // wide, step, 0)

    block = lax.div(q * half, BLOCK)
    weight = cov[v, block, 0].astype(F32)
    count = jnp.float32(0.0)
    for n in range(4):
        count = count + cov[n, block, 0].astype(F32)

    across_arrive(first, 0)
    for j in range(2):
        for c in range(2):
            spread_arrive(first, 0, c, j)
            if (j, c) == (1, 1):
                spread_start(view_copies)
            for h in range(quarter // group):
                forward(first, c * slab + j * quarter + group * h)

    lay_views.wait()
    across_arrive(vext, 5)
    blank = jnp.zeros((slab * half, width), F32)
    data[: slab * half, :] = blank
    data[(slab + planes) * half :, :] = blank
    row = lax.broadcasted_iota(jnp.int32, (half, 3 * half), 0)
    col = lax.broadcasted_iota(jnp.int32, (half, 3 * half), 1)
    pick_rows = (col == row + half + shifts[0, 1]).astype(F32).astype(BF16)
    row = lax.broadcasted_iota(jnp.int32, (width, width), 0)
    col = lax.broadcasted_iota(jnp.int32, (width, width), 1)
    pick_x = (row == col + shifts[0, 2]).astype(F32).astype(BF16)

    def window(plane):
        parts = []
        for j in range(0, group, 2):
            pair = jnp.concatenate([vext[plane + j], vext[plane + j + 1]], axis=1)
            both = dot(pick_rows, pair)
            parts += [both[:, :width], both[:, width:]]
        moved = dot(jnp.concatenate(parts, axis=0).astype(BF16), pick_x)
        data[(slab + plane) * half : (slab + plane + group) * half, :] = moved

    for j in range(2):
        for c in range(2):
            spread_arrive(vext, 5, c, j)
            for h in range(quarter // group):
                window(c * slab + j * quarter + group * h)

    shifted = (slab + shifts[0, 0]) * half

    def column(ref, y):
        return jnp.concatenate(
            [ref[pl.ds(y, planes, stride=half), :], ref[pl.ds(y + 1, planes, stride=half), :]],
            axis=1,
        )

    def along_planes(i):
        for j in range(0, 4, 2):
            y = 4 * i + j
            both = dot(zmat[0], column(mid, y).astype(BF16))
            predicted = both[:planes] + both[planes:]
            ratio = column(data, y + shifted) / (predicted + 0.05)
            both = dot(zmat[1], ratio.astype(BF16))
            both = both[:planes] + both[planes:]
            back[pl.ds(y, planes, stride=half), :] = both[:, :width]
            back[pl.ds(y + 1, planes, stride=half), :] = both[:, width:]

    pieces = group * half
    order = ((3, 0), (3, 1), (1, 0), (2, 1), (1, 1), (2, 0), (0, 0), (0, 1))
    place_rows = pl.ds(pl.multiple_of(half * g, half), half)
    halos, sends, results = [], [], []

    for step in range(ITERS):
        loop(half // 4, along_planes, 2)
        ext = bext.at[step]
        last = step == ITERS - 1
        copies = {}
        for k, h in order:
            part = piece(k, h)
            at = pl.multiple_of((quarter * other_view(k) + group * h) * half, pieces)
            ext[part, half : 2 * half, :] = (
                back[pl.ds(at, pieces), :].reshape(group, half, width).astype(BF16)
            )
            copies[k, h] = halo(ext, 11 + 16 * step, k, h)
            halo_start(copies[k, h])
        halos += list(copies.values())
        base = 59 + 6 * step
        sums = {}
        for h in range(2):
            sums[3, h] = remote(
                term.at[step, h], relay.at[step, h], base + h, base + h,
                (other_view(1 + h), s, g),
            )
            for k in (1, 2):
                at = base + 2 * k + h
                sums[k, h] = remote(
                    term.at[step, 2 * k + h], slots.at[step, k - 1, h], at, at,
                    (other_view(k), s, g),
                )
        sends += list(sums.values())
        for k, h in order:
            halo_arrive(copies[k, h])
            value = weight * backward(ext, quarter * other_view(k) + group * h)
            if k == 0:
                own[h] = value
                continue
            if (k, h) in ((1, 1), (2, 0)):
                sums[3, h].wait_recv()
                value = value + relay[step, h]
            term[step, h if k == 3 else 2 * k + h] = value
            sums[k, h].start()
        if step == 0:

            @pl.when(g != va)
            def _():
                mast_copy.wait_recv()

        here = quarter * v
        ext = None if last else fext.at[step + 1]
        news, copies = {}, {}
        for h in range(2):
            sums[1, h].wait_recv()
            sums[2, h].wait_recv()
            total = own[h] + slots[step, 0, h] + slots[step, 1, h]
            at = slice(group * h, group * (h + 1))
            field = mast[at] * total.reshape(group, half, width) / count
            if last:
                fin[at] = field
                place = out.at[
                    pl.ds(pl.multiple_of(quarter * vb + group * h, group), group), place_rows, :
                ]
                arrive = 77 + 4 * vb + 2 * g + h
                copies = [
                    remote(fin.at[at], place, 77 + 2 * k + h, arrive, (other_view(k), s, va))
                    for k in range(3)
                ]
                copies[1].start()
                copies[2].start()
                sends += copies[1:]
                results.append((copies[0], pltpu.make_async_copy(fin.at[at], place, local.at[h])))

                @pl.when(g == va)
                def _():
                    results[-1][1].start()

                @pl.when(g != va)
                def _():
                    results[-1][0].start()

                continue
            mast[at] = field
            part = piece(0, h)
            ext[part, half : 2 * half, :] = field.astype(BF16)
            src = ext.at[part, half : 2 * half, :]
            for k in (1, 2):
                at = 71 + 2 * (k - 1) + h
                sent = remote(src, src, at, at, (other_view(k), s, g))
                sent.start()
                sends.append(sent)
            copies[0, h] = halo(ext, 43, 0, h)
            halo_start(copies[0, h])
        if last:
            break

        def gathered(k, h):
            src = ext.at[piece(k, h), half : 2 * half, :]
            at = 71 + 2 * (k - 1) + h
            remote(src, src, at, at, sibling).wait_recv()
            if (k, h) in ((1, 0), (2, 1)):
                sent = remote(src, src, 75 + h, 75 + h, (other_view(3 - k), s, g))
                sent.start()
                sends.append(sent)
            copies[k, h] = halo(ext, 43, k, h)
            halo_start(copies[k, h])

        def blurred(k, h):
            halo_arrive(copies[k, h])
            forward(ext, quarter * other_view(k) + group * h)

        for k, h in ((1, 0), (2, 0), (1, 1), (2, 1)):
            gathered(k, h)
        blurred(0, 0)
        blurred(0, 1)
        gathered(3, 0)
        blurred(1, 0)
        blurred(2, 0)
        gathered(3, 1)
        for k, h in ((1, 1), (2, 1), (3, 0), (3, 1)):
            blurred(k, h)
        halos += list(copies.values())

    same = 1 - lax.rem(g + va, 2)
    from_b = lax.rem(vb + same, 2)
    from_h = 1 - same
    onward = 2 * lax.rem(va + same, 2) + lax.rem(vb + 1 - same, 2)

    def spot(b, c, h):
        first_plane = pl.multiple_of(quarter * b + group * h, group)
        return out.at[pl.ds(first_plane, group), half * c : half * (c + 1), :]

    for c in range(2):
        at = 77 + 4 * from_b + 2 * c + from_h
        target = spot(from_b, c, from_h)
        sent = remote(target, target, 83 + c, at, (onward, s, g))
        sent.wait_recv()
        sent.start()
        sends.append(sent)
    for h in range(2):
        for b in range(2):
            for c in range(2):
                itself = jnp.logical_and(v == 2 * g + b, g == c)
                done = jnp.logical_and(from_b == b, from_h == h)

                @pl.when(jnp.logical_not(jnp.logical_or(itself, done)))
                def _():
                    target = spot(b, c, h)
                    at = 77 + 4 * b + 2 * c + h
                    remote(target, target, at, at, sibling).wait_recv()

    @pl.when(g == va)
    def _():
        mast_copy.wait_send()
        for _, copy in results:
            copy.wait()

    @pl.when(g != va)
    def _():
        for copy, _ in results:
            copy.wait_send()

    spread_sent(est_copies)
    spread_sent(view_copies)
    for copies in halos:
        halo_sent(copies)
    for sent in sends:
        sent.wait_send()


def on_device(strips, estimate, views, shifts, kernels, coverage):
    slab, strip, width = estimate.shape
    half, planes = strip // 2, 2 * slab
    quarter = planes // 4
    hbm = pl.BlockSpec(memory_space=pl.ANY)
    smem = pl.BlockSpec(memory_space=pltpu.SMEM)
    rows = planes * half
    scratch = [
        pltpu.VMEM(estimate.shape, F32),
        pltpu.VMEM((ITERS, planes, 3 * half, width), BF16),
        pltpu.VMEM((ITERS, planes, 3 * half, width), BF16),
        pltpu.VMEM((planes, 3 * half, width), BF16),
        pltpu.VMEM((2 * rows, width), F32),
        pltpu.VMEM((rows, width), F32),
        pltpu.VMEM((rows, width), F32),
        pltpu.VMEM((quarter, half, width), F32),
        pltpu.VMEM((2, quarter * half // 2, width), F32),
        pltpu.VMEM((ITERS, 6, quarter * half // 2, width), F32),
        pltpu.VMEM((ITERS, 2, 2, quarter * half // 2, width), F32),
        pltpu.VMEM((ITERS, 2, quarter * half // 2, width), F32),
        pltpu.VMEM((quarter, half, width), F32),
        pltpu.VMEM((2, 2 * half, 3 * half), BF16),
        pltpu.VMEM((width, 2 * width), BF16),
        pltpu.VMEM((2 * width, 2 * width), BF16),
        pltpu.VMEM((2, 2 * planes, planes), BF16),
        pltpu.SemaphoreType.DMA((85,)),
        pltpu.SemaphoreType.DMA((85,)),
        pltpu.SemaphoreType.DMA((2,)),
    ]
    return pl.pallas_call(
        functools.partial(kernel, strips),
        out_shape=jax.ShapeDtypeStruct(estimate.shape, F32),
        in_specs=[smem, smem, smem, hbm, hbm],
        out_specs=hbm,
        scratch_shapes=scratch,
        compiler_params=pltpu.CompilerParams(
            collective_id=0, has_side_effects=True, vmem_limit_bytes=62 * 1024 * 1024
        ),
        cost_estimate=pl.CostEstimate(
            flops=12 * 2 * rows * width * 100, bytes_accessed=8 * rows * width, transcendentals=0
        ),
    )(coverage, shifts, kernels, estimate, views)


def solution(mesh):
    placed = (
        P("gz", "xy", None),
        P("view", "gz", "xy", None),
        P("view", None),
        P("view", None, None),
        P(),
    )
    return jax.shard_map(
        functools.partial(on_device, mesh.shape["xy"]),
        mesh=mesh, in_specs=placed, out_specs=P("gz", "xy", None), check_vma=False,
    )
```

```python
import functools

import jax
import jax.numpy as jnp
from jax import lax
from jax.experimental import pallas as pl
from jax.experimental.pallas import tpu as pltpu
from jax.sharding import PartitionSpec as P

BLOCK = 128
ITERS = 2
MESH = pl.DeviceIdType.MESH
F32 = jnp.float32
BF16 = jnp.bfloat16


def split(value):
    high = value.astype(BF16)
    return high, (value - high.astype(F32)).astype(BF16)


def encode(value):
    groups = value.reshape(-1, 8, value.shape[-1])
    top = jnp.maximum(jnp.max(groups, axis=0), 1e-30)
    whole = (groups * (32767.0 / top)[None] + 0.5).astype(jnp.int32)
    return whole.reshape(value.shape).astype(jnp.int16), top


def decode(code, top):
    groups = code.astype(jnp.int32).astype(F32).reshape(-1, 8, code.shape[-1])
    return (groups * (top * (1.0 / 32767.0))[None]).reshape(code.shape)


class Pair:
    def __init__(self, *copies):
        self.copies = copies

    def start(self):
        for copy in self.copies:
            copy.start()

    def wait_recv(self):
        for copy in self.copies:
            copy.wait_recv()

    def wait_send(self):
        for copy in self.copies:
            copy.wait_send()


def dot(a, b):
    return jnp.dot(a, b, preferred_element_type=F32)


def band(kern, axis, forms):
    marks = []
    for rows, cols, sign, base in forms:
        row = lax.broadcasted_iota(jnp.int32, (rows, cols), 0)
        col = lax.broadcasted_iota(jnp.int32, (rows, cols), 1)
        marks.append(base + sign * (row - col))

    def add_tap(tap, carry):
        total, mats = carry
        value = kern[axis, 0, tap]
        return total + value, tuple(
            mat + jnp.where(mark == tap, value, 0.0) for mat, mark in zip(mats, marks)
        )

    zeros = tuple(jnp.zeros(mark.shape, F32) for mark in marks)
    total, mats = lax.fori_loop(0, kern.shape[2], add_tap, (jnp.float32(0.0), zeros))
    return [mat / total for mat in mats]


def kernel(
    strips, cov, shifts, kern, given, views, out,
    est, fext, bext, vext, data, mid, back, mast, own, term, term_top, inbox, inbox_top,
    fin, fin_top, final, final_top,
    rmat, xfor, xback, zmat, send, recv, send_top, recv_top, local,
):
    slab, strip, width = est.shape
    half = strip // 2
    planes = 2 * slab
    taps = kern.shape[2]
    reach = (taps - 1) // 2
    quarter = planes // 4
    group = quarter // 2
    v, s, g = lax.axis_index("view"), lax.axis_index("xy"), lax.axis_index("gz")
    va, vb = lax.div(v, 2), lax.rem(v, 2)
    q = 2 * s + g
    has_prev, has_next = q > 0, q < 2 * strips - 1

    def other_view(k):
        return lax.rem(va + k // 2, 2) * 2 + lax.rem(vb + k % 2, 2)

    fetch = pltpu.make_async_copy(given, est, local.at[0])
    fetch.start()
    sibling = (v, s, 1 - g)
    before = (v, lax.rem(s - 1 + g + strips, strips), 1 - g)
    after = (v, lax.rem(s + g, strips), 1 - g)
    strip_before = lax.rem(s - 1 + strips, strips)
    strip_after = lax.rem(s + 1, strips)

    barrier = pltpu.get_barrier_semaphore()

    def greet(device):
        pl.semaphore_signal(barrier, inc=1, device_id=device, device_id_type=MESH)

    greet(sibling)
    for k in range(1, 4):
        greet((other_view(k), s, g))
        greet((other_view(k), s, 1 - g))

    @pl.when(s > 0)
    def _():
        greet((v, strip_before, 0))
        greet((v, strip_before, 1))

    @pl.when(s < strips - 1)
    def _():
        greet((v, strip_after, 0))
        greet((v, strip_after, 1))

    def remote(src, dst, send_id, recv_id, device):
        return pltpu.make_async_remote_copy(
            src_ref=src, dst_ref=dst, send_sem=send.at[send_id], recv_sem=recv.at[recv_id],
            device_id=device, device_id_type=MESH,
        )

    def coded(src, src_top, dst, dst_top, send_id, recv_id, device):
        return Pair(
            remote(src, dst, send_id, recv_id, device),
            pltpu.make_async_remote_copy(
                src_ref=src_top, dst_ref=dst_top, send_sem=send_top.at[send_id],
                recv_sem=recv_top.at[recv_id], device_id=device, device_id_type=MESH,
            ),
        )

    mine = pl.ds(pl.multiple_of(slab * g, slab), slab)
    lay = pl.multiple_of(half - half * g, half)
    first = fext.at[0]

    lay_views = pltpu.make_async_copy(
        views.at[0], vext.at[mine, pl.ds(lay, strip), :], local.at[1]
    )
    lay_views.start()

    @pl.when(q == 0)
    def _():
        vext[:, 0:half, :] = jnp.zeros((planes, half, width), BF16)
        for n in range(ITERS):
            fext[n, :, 0:half, :] = jnp.zeros((planes, half, width), BF16)
            bext[n, :, 0:half, :] = jnp.zeros((planes, half, width), BF16)

    @pl.when(q == 2 * strips - 1)
    def _():
        vext[:, 2 * half :, :] = jnp.zeros((planes, half, width), BF16)
        for n in range(ITERS):
            fext[n, :, 2 * half :, :] = jnp.zeros((planes, half, width), BF16)
            bext[n, :, 2 * half :, :] = jnp.zeros((planes, half, width), BF16)

    fetch.wait()
    for i in range(0, slab, group):
        first[pl.ds(slab * g + i, group), pl.ds(lay, strip), :] = est[i : i + group].astype(BF16)

    pl.semaphore_wait(
        barrier, 7 + 2 * (s > 0).astype(jnp.int32) + 2 * (s < strips - 1).astype(jnp.int32)
    )

    def spread(ext, base, block):
        across = remote(
            block,
            ext.at[mine, pl.ds(pl.multiple_of(half * g, half), strip), :],
            base, base, sibling,
        )
        down, up = [], []
        for j in range(2):
            src = block.at[quarter * j : quarter * (j + 1)]
            part = pl.ds(pl.multiple_of(slab * g + quarter * j, quarter), quarter)
            down.append(
                remote(
                    src.at[:, 0:half, :], ext.at[part, 2 * half : 3 * half, :],
                    base + 1 + j, base + 1 + 2 * g + j, (v, strip_before, 1),
                )
            )
            up.append(
                remote(
                    src.at[:, half:strip, :], ext.at[part, 0:half, :],
                    base + 3 + j, base + 1 + 2 * g + j, (v, strip_after, 0),
                )
            )
        return across, down, up

    def spread_start(copies):
        across, down, up = copies

        @pl.when(s > 0)
        def _():
            for copy in down:
                copy.start()

        @pl.when(s < strips - 1)
        def _():
            for copy in up:
                copy.start()

        across.start()

    def across_arrive(ext, base):
        theirs = pl.ds(pl.multiple_of(slab * (1 - g), slab), slab)
        remote(
            ext.at[mine, pl.ds(lay, strip), :], ext.at[theirs, pl.ds(lay, strip), :],
            base, base, sibling,
        ).wait_recv()

    def spread_arrive(ext, base, c, j):
        part = pl.ds(c * slab + j * quarter, quarter)
        number = base + 1 + 2 * c + j

        @pl.when(jnp.logical_and(g == 0, s > 0))
        def _():
            remote(
                ext.at[part, half : 2 * half, :], ext.at[part, 0:half, :],
                number, number, sibling,
            ).wait_recv()

        @pl.when(jnp.logical_and(g == 1, s < strips - 1))
        def _():
            remote(
                ext.at[part, half : 2 * half, :], ext.at[part, 2 * half : 3 * half, :],
                number, number, sibling,
            ).wait_recv()

    def spread_sent(copies):
        across, down, up = copies
        across.wait_send()

        @pl.when(s > 0)
        def _():
            for copy in down:
                copy.wait_send()

        @pl.when(s < strips - 1)
        def _():
            for copy in up:
                copy.wait_send()

    est_copies = spread(first, 0, first.at[mine, pl.ds(lay, strip), :])
    spread_start(est_copies)
    view_copies = spread(vext, 5, views.at[0])
    quarter_here = pl.ds(pl.multiple_of(quarter * vb, quarter), quarter)
    mast_copy = remote(
        est.at[quarter_here, pl.ds(pl.multiple_of(half * (1 - g), half), half), :],
        mast, 10, 10, sibling,
    )

    @pl.when(g == va)
    def _():
        mast_copy.start()
        mast[...] = est[quarter_here, pl.ds(pl.multiple_of(half * g, half), half), :]

    x_forward, = band(kern, 2, [(width, width, 1, reach)])
    x_backward, = band(kern, 2, [(width, width, -1, reach)])
    high, low = split(x_forward)
    xfor[:, :width] = high
    xfor[:, width:] = low
    high, low = split(x_backward)
    xback[:width, :width] = high
    xback[:width, width:] = low
    xback[width:, :width] = high
    xback[width:, width:] = jnp.zeros((width, width), BF16)
    z_mats = band(kern, 0, [(planes, planes, -1, reach), (planes, planes, 1, reach)])
    r_mats = band(
        kern, 1, [(half, 3 * half, -1, reach - half), (half, 3 * half, 1, reach + half)]
    )
    for way in range(2):
        high, low = split(z_mats[way])
        zmat[way, :planes, :] = high
        zmat[way, planes:, :] = low
        high, low = split(r_mats[way])
        rmat[way, :half, :] = high
        rmat[way, half:, :] = low

    def piece(k, h):
        return pl.ds(pl.multiple_of(quarter * other_view(k) + group * h, group), group)

    def halo(ext, base, k, h):
        part = piece(k, h)
        src = ext.at[part, half : 2 * half, :]
        at = base + 4 * k + 2 * h
        return (
            remote(src, ext.at[part, 2 * half : 3 * half, :], at, at, before),
            remote(src, ext.at[part, 0:half, :], at + 1, at + 1, after),
        )

    def halo_start(copies):
        down, up = copies

        @pl.when(has_prev)
        def _():
            down.start()

        @pl.when(has_next)
        def _():
            up.start()

    def halo_arrive(copies):
        down, up = copies

        @pl.when(has_next)
        def _():
            down.wait_recv()

        @pl.when(has_prev)
        def _():
            up.wait_recv()

    def halo_sent(copies):
        down, up = copies

        @pl.when(has_prev)
        def _():
            down.wait_send()

        @pl.when(has_next)
        def _():
            up.wait_send()

    def along_rows(ext, way, plane):
        mat = rmat[way]
        parts = []
        for i in range(0, group, 2):
            both = dot(mat, jnp.concatenate([ext[plane + i], ext[plane + i + 1]], axis=1))
            both = both[:half] + both[half:]
            parts += [both[:, :width], both[:, width:]]
        return jnp.concatenate(parts, axis=0)

    def forward(ext, plane):
        both = dot(along_rows(ext, 0, plane).astype(BF16), xfor[...])
        mid[pl.ds(pl.multiple_of(plane * half, group * half), group * half), :] = (
            both[:, :width] + both[:, width:]
        )

    def backward(ext, plane):
        high, low = split(along_rows(ext, 1, plane))
        both = dot(jnp.concatenate([high, low], axis=1), xback[...])
        return both[:, :width] + both[:, width:]

    def loop(steps, body, wide=1):
        def step(i, carry):
            for n in range(wide):
                body(wide * i + n)
            return carry

        lax.fori_loop(0, steps // wide, step, 0)

    block = lax.div(q * half, BLOCK)
    weight = cov[block, 0, v].astype(F32)
    count = jnp.float32(0.0)
    for n in range(4):
        count = count + cov[block, 0, n].astype(F32)

    across_arrive(first, 0)
    for j in range(2):
        for c in range(2):
            spread_arrive(first, 0, c, j)
            if (j, c) == (1, 1):
                spread_start(view_copies)
            for h in range(quarter // group):
                forward(first, c * slab + j * quarter + group * h)

    lay_views.wait()
    across_arrive(vext, 5)
    blank = jnp.zeros((slab * half, width), F32)
    data[: slab * half, :] = blank
    data[(slab + planes) * half :, :] = blank
    row = lax.broadcasted_iota(jnp.int32, (half, 3 * half), 0)
    col = lax.broadcasted_iota(jnp.int32, (half, 3 * half), 1)
    pick_rows = (col == row + half + shifts[0, 1]).astype(F32).astype(BF16)
    row = lax.broadcasted_iota(jnp.int32, (width, width), 0)
    col = lax.broadcasted_iota(jnp.int32, (width, width), 1)
    pick_x = (row == col + shifts[0, 2]).astype(F32).astype(BF16)

    def window(plane):
        parts = []
        for j in range(0, group, 2):
            pair = jnp.concatenate([vext[plane + j], vext[plane + j + 1]], axis=1)
            both = dot(pick_rows, pair)
            parts += [both[:, :width], both[:, width:]]
        moved = dot(jnp.concatenate(parts, axis=0).astype(BF16), pick_x)
        data[(slab + plane) * half : (slab + plane + group) * half, :] = moved

    for j in range(2):
        for c in range(2):
            spread_arrive(vext, 5, c, j)
            for h in range(quarter // group):
                window(c * slab + j * quarter + group * h)

    shifted = (slab + shifts[0, 0]) * half

    def column(ref, y):
        return jnp.concatenate(
            [ref[pl.ds(y, planes, stride=half), :], ref[pl.ds(y + 1, planes, stride=half), :]],
            axis=1,
        )

    def along_planes(i):
        for j in range(0, 4, 2):
            y = 4 * i + j
            both = dot(zmat[0], column(mid, y).astype(BF16))
            predicted = both[:planes] + both[planes:]
            ratio = column(data, y + shifted) / (predicted + 0.05)
            both = dot(zmat[1], ratio.astype(BF16))
            both = both[:planes] + both[planes:]
            back[pl.ds(y, planes, stride=half), :] = both[:, :width]
            back[pl.ds(y + 1, planes, stride=half), :] = both[:, width:]

    pieces = group * half
    order = ((3, 0), (3, 1), (1, 0), (2, 1), (1, 1), (2, 0), (0, 0), (0, 1))
    halos, sends, results = [], [], []

    for step in range(ITERS):
        loop(half // 4, along_planes, 2)
        ext = bext.at[step]
        last = step == ITERS - 1
        copies = {}
        for k, h in order:
            part = piece(k, h)
            at = pl.multiple_of((quarter * other_view(k) + group * h) * half, pieces)
            ext[part, half : 2 * half, :] = (
                back[pl.ds(at, pieces), :].reshape(group, half, width).astype(BF16)
            )
            copies[k, h] = halo(ext, 11 + 16 * step, k, h)
            halo_start(copies[k, h])
        halos += list(copies.values())
        base = 59 + 6 * step
        sums = {}
        for k in (3, 1, 2):
            for h in range(2):
                n = h if k == 3 else 2 * k + h
                sums[k, h] = coded(
                    term.at[step, n], term_top.at[step, n],
                    inbox.at[step, n], inbox_top.at[step, n],
                    base + n, base + n, (other_view(1 + h if k == 3 else k), s, g),
                )
        sends += list(sums.values())
        for k, h in order:
            halo_arrive(copies[k, h])
            value = weight * backward(ext, quarter * other_view(k) + group * h)
            if k == 0:
                own[h] = value
                continue
            if (k, h) in ((1, 1), (2, 0)):
                sums[3, h].wait_recv()
                value = value + decode(inbox[step, h], inbox_top[step, h])
            n = h if k == 3 else 2 * k + h
            term[step, n], term_top[step, n] = encode(value)
            sums[k, h].start()
        if step == 0:

            @pl.when(g != va)
            def _():
                mast_copy.wait_recv()

        here = quarter * v
        ext = None if last else fext.at[step + 1]
        news, copies = {}, {}
        for h in range(2):
            sums[1, h].wait_recv()
            sums[2, h].wait_recv()
            total = own[h]
            for n in (2 + h, 4 + h):
                total = total + decode(inbox[step, n], inbox_top[step, n])
            at = slice(group * h, group * (h + 1))
            field = mast[at] * total.reshape(group, half, width) / count
            if last:
                fin[h], fin_top[h] = encode(field.reshape(pieces, width))
                n = 4 * vb + 2 * g + h
                copies = [
                    coded(
                        fin.at[h], fin_top.at[h], final.at[n], final_top.at[n],
                        77 + 2 * k + h, 77 + n, (other_view(k), s, va),
                    )
                    for k in range(3)
                ]
                copies[1].start()
                copies[2].start()
                sends += copies[1:]
                results.append(copies[0])

                @pl.when(g != va)
                def _():
                    results[-1].start()

                continue
            mast[at] = field
            part = piece(0, h)
            ext[part, half : 2 * half, :] = field.astype(BF16)
            src = ext.at[part, half : 2 * half, :]
            for k in (1, 2):
                at = 71 + 2 * (k - 1) + h
                sent = remote(src, src, at, at, (other_view(k), s, g))
                sent.start()
                sends.append(sent)
            copies[0, h] = halo(ext, 43, 0, h)
            halo_start(copies[0, h])
        if last:
            break

        def gathered(k, h):
            src = ext.at[piece(k, h), half : 2 * half, :]
            at = 71 + 2 * (k - 1) + h
            remote(src, src, at, at, sibling).wait_recv()
            if (k, h) in ((1, 0), (2, 1)):
                sent = remote(src, src, 75 + h, 75 + h, (other_view(3 - k), s, g))
                sent.start()
                sends.append(sent)
            copies[k, h] = halo(ext, 43, k, h)
            halo_start(copies[k, h])

        def blurred(k, h):
            halo_arrive(copies[k, h])
            forward(ext, quarter * other_view(k) + group * h)

        for k, h in ((1, 0), (2, 0), (1, 1), (2, 1)):
            gathered(k, h)
        blurred(0, 0)
        blurred(0, 1)
        gathered(3, 0)
        blurred(1, 0)
        blurred(2, 0)
        gathered(3, 1)
        for k, h in ((1, 1), (2, 1), (3, 0), (3, 1)):
            blurred(k, h)
        halos += list(copies.values())

    same = 1 - lax.rem(g + va, 2)
    from_b = lax.rem(vb + same, 2)
    from_h = 1 - same
    onward = 2 * lax.rem(va + same, 2) + lax.rem(vb + 1 - same, 2)

    for c in range(2):
        n = 4 * from_b + 2 * c + from_h
        sent = coded(
            final.at[n], final_top.at[n], final.at[n], final_top.at[n],
            83 + c, 77 + n, (onward, s, g),
        )
        sent.wait_recv()
        sent.start()
        sends.append(sent)
    for h in range(2):
        for b in range(2):
            for c in range(2):
                n = 4 * b + 2 * c + h
                itself = jnp.logical_and(v == 2 * g + b, g == c)
                done = jnp.logical_and(from_b == b, from_h == h)

                def place(code, top):
                    first_plane = quarter * b + group * h
                    out[first_plane : first_plane + group, half * c : half * (c + 1), :] = decode(
                        code, top
                    ).reshape(group, half, width)

                @pl.when(jnp.logical_not(jnp.logical_or(itself, done)))
                def _():
                    coded(
                        final.at[n], final_top.at[n], final.at[n], final_top.at[n],
                        77 + n, 77 + n, sibling,
                    ).wait_recv()

                @pl.when(itself)
                def _():
                    place(fin[h], fin_top[h])

                @pl.when(jnp.logical_not(itself))
                def _():
                    place(final[n], final_top[n])

    @pl.when(g == va)
    def _():
        mast_copy.wait_send()

    @pl.when(g != va)
    def _():
        for copy in results:
            copy.wait_send()

    spread_sent(est_copies)
    spread_sent(view_copies)
    for copies in halos:
        halo_sent(copies)
    for sent in sends:
        sent.wait_send()


def on_device(strips, estimate, views, shifts, kernels, coverage):
    slab, strip, width = estimate.shape
    half, planes = strip // 2, 2 * slab
    quarter = planes // 4
    hbm = pl.BlockSpec(memory_space=pltpu.HBM)
    smem = pl.BlockSpec(memory_space=pltpu.SMEM)
    rows = planes * half
    scratch = [
        pltpu.VMEM(estimate.shape, F32),
        pltpu.VMEM((ITERS, planes, 3 * half, width), BF16),
        pltpu.VMEM((ITERS, planes, 3 * half, width), BF16),
        pltpu.VMEM((planes, 3 * half, width), BF16),
        pltpu.VMEM((2 * rows, width), F32),
        pltpu.VMEM((rows, width), F32),
        pltpu.VMEM((rows, width), F32),
        pltpu.VMEM((quarter, half, width), F32),
        pltpu.VMEM((2, quarter * half // 2, width), F32),
        pltpu.VMEM((ITERS, 6, quarter * half // 2, width), jnp.int16),
        pltpu.VMEM((ITERS, 6, 8, width), F32),
        pltpu.VMEM((ITERS, 6, quarter * half // 2, width), jnp.int16),
        pltpu.VMEM((ITERS, 6, 8, width), F32),
        pltpu.VMEM((2, quarter * half // 2, width), jnp.int16),
        pltpu.VMEM((2, 8, width), F32),
        pltpu.VMEM((8, quarter * half // 2, width), jnp.int16),
        pltpu.VMEM((8, 8, width), F32),
        pltpu.VMEM((2, 2 * half, 3 * half), BF16),
        pltpu.VMEM((width, 2 * width), BF16),
        pltpu.VMEM((2 * width, 2 * width), BF16),
        pltpu.VMEM((2, 2 * planes, planes), BF16),
        pltpu.SemaphoreType.DMA((85,)),
        pltpu.SemaphoreType.DMA((85,)),
        pltpu.SemaphoreType.DMA((85,)),
        pltpu.SemaphoreType.DMA((85,)),
        pltpu.SemaphoreType.DMA((2,)),
    ]
    return pl.pallas_call(
        functools.partial(kernel, strips),
        out_shape=jax.ShapeDtypeStruct(estimate.shape, F32),
        in_specs=[smem, smem, smem, hbm, hbm],
        out_specs=pl.BlockSpec(memory_space=pltpu.VMEM),
        scratch_shapes=scratch,
        compiler_params=pltpu.CompilerParams(
            collective_id=0, has_side_effects=True, vmem_limit_bytes=40 * 1024 * 1024
        ),
        cost_estimate=pl.CostEstimate(
            flops=12 * 2 * rows * width * 100, bytes_accessed=8 * rows * width, transcendentals=0
        ),
    )(coverage.transpose(1, 2, 0), shifts, kernels.transpose(1, 0, 2), estimate, views)


def solution(mesh):
    placed = (
        P("gz", "xy", None),
        P("view", "gz", "xy", None),
        P("view", None),
        P("view", None, None),
        P(),
    )
    return jax.shard_map(
        functools.partial(on_device, mesh.shape["xy"]),
        mesh=mesh, in_specs=placed, out_specs=P("gz", "xy", None), check_vma=False,
    )
```

```python
import functools

import jax
import jax.numpy as jnp
from jax import lax
from jax.experimental import pallas as pl
from jax.experimental.pallas import tpu as pltpu
from jax.sharding import PartitionSpec as P

BLOCK = 128
ITERS = 2
MESH = pl.DeviceIdType.MESH
F32 = jnp.float32
BF16 = jnp.bfloat16


def split(value):
    high = value.astype(BF16)
    return high, (value - high.astype(F32)).astype(BF16)


def encode(value):
    groups = value.reshape(-1, 8, value.shape[-1])
    top = jnp.maximum(jnp.max(groups, axis=0), 1e-30)
    whole = (groups * (32767.0 / top)[None] + 0.5).astype(jnp.int32)
    return whole.reshape(value.shape).astype(jnp.int16), top


def decode(code, top):
    groups = code.astype(jnp.int32).astype(F32).reshape(-1, 8, code.shape[-1])
    return (groups * (top * (1.0 / 32767.0))[None]).reshape(code.shape)


class Pair:
    def __init__(self, *copies):
        self.copies = copies

    def start(self):
        for copy in self.copies:
            copy.start()

    def wait_recv(self):
        for copy in self.copies:
            copy.wait_recv()

    def wait_send(self):
        for copy in self.copies:
            copy.wait_send()


def dot(a, b):
    return jnp.dot(a, b, preferred_element_type=F32)


def band(kern, axis, forms):
    marks = []
    for rows, cols, sign, base in forms:
        row = lax.broadcasted_iota(jnp.int32, (rows, cols), 0)
        col = lax.broadcasted_iota(jnp.int32, (rows, cols), 1)
        marks.append(base + sign * (row - col))

    def add_tap(tap, carry):
        total, mats = carry
        value = kern[axis, 0, tap]
        return total + value, tuple(
            mat + jnp.where(mark == tap, value, 0.0) for mat, mark in zip(mats, marks)
        )

    zeros = tuple(jnp.zeros(mark.shape, F32) for mark in marks)
    total, mats = lax.fori_loop(0, kern.shape[2], add_tap, (jnp.float32(0.0), zeros))
    return [mat / total for mat in mats]


def kernel(
    strips, cov, shifts, kern, given, views, out,
    est, fext, bext, vext, data, mid, back, mast, own, term, term_top, inbox, inbox_top,
    fin, fin_top, final, final_top,
    rmat, xfor, xback, zmat, send, recv, send_top, recv_top, local,
):
    slab, strip, width = est.shape
    half = strip // 2
    planes = 2 * slab
    taps = kern.shape[2]
    reach = (taps - 1) // 2
    quarter = planes // 4
    group = quarter // 2
    v, s, g = lax.axis_index("view"), lax.axis_index("xy"), lax.axis_index("gz")
    va, vb = lax.div(v, 2), lax.rem(v, 2)
    q = 2 * s + g
    has_prev, has_next = q > 0, q < 2 * strips - 1

    def other_view(k):
        return lax.rem(va + k // 2, 2) * 2 + lax.rem(vb + k % 2, 2)

    fetch = pltpu.make_async_copy(given, est, local.at[0])
    fetch.start()
    sibling = (v, s, 1 - g)
    before = (v, lax.rem(s - 1 + g + strips, strips), 1 - g)
    after = (v, lax.rem(s + g, strips), 1 - g)
    strip_before = lax.rem(s - 1 + strips, strips)
    strip_after = lax.rem(s + 1, strips)

    barrier = pltpu.get_barrier_semaphore()

    def greet(device):
        pl.semaphore_signal(barrier, inc=1, device_id=device, device_id_type=MESH)

    greet(sibling)
    for k in range(1, 4):
        greet((other_view(k), s, g))
        greet((other_view(k), s, 1 - g))

    @pl.when(s > 0)
    def _():
        greet((v, strip_before, 0))
        greet((v, strip_before, 1))

    @pl.when(s < strips - 1)
    def _():
        greet((v, strip_after, 0))
        greet((v, strip_after, 1))

    def remote(src, dst, send_id, recv_id, device):
        return pltpu.make_async_remote_copy(
            src_ref=src, dst_ref=dst, send_sem=send.at[send_id], recv_sem=recv.at[recv_id],
            device_id=device, device_id_type=MESH,
        )

    def coded(src, src_top, dst, dst_top, send_id, recv_id, device):
        return Pair(
            remote(src, dst, send_id, recv_id, device),
            pltpu.make_async_remote_copy(
                src_ref=src_top, dst_ref=dst_top, send_sem=send_top.at[send_id],
                recv_sem=recv_top.at[recv_id], device_id=device, device_id_type=MESH,
            ),
        )

    mine = pl.ds(pl.multiple_of(slab * g, slab), slab)
    lay = pl.multiple_of(half - half * g, half)
    first = fext.at[0]

    lay_views = pltpu.make_async_copy(
        views.at[0], vext.at[mine, pl.ds(lay, strip), :], local.at[1]
    )
    lay_views.start()

    @pl.when(q == 0)
    def _():
        vext[:, 0:half, :] = jnp.zeros((planes, half, width), BF16)
        for n in range(ITERS):
            fext[n, :, 0:half, :] = jnp.zeros((planes, half, width), BF16)
            bext[n, :, 0:half, :] = jnp.zeros((planes, half, width), BF16)

    @pl.when(q == 2 * strips - 1)
    def _():
        vext[:, 2 * half :, :] = jnp.zeros((planes, half, width), BF16)
        for n in range(ITERS):
            fext[n, :, 2 * half :, :] = jnp.zeros((planes, half, width), BF16)
            bext[n, :, 2 * half :, :] = jnp.zeros((planes, half, width), BF16)

    fetch.wait()
    for i in range(0, slab, group):
        first[pl.ds(slab * g + i, group), pl.ds(lay, strip), :] = est[i : i + group].astype(BF16)

    pl.semaphore_wait(
        barrier, 7 + 2 * (s > 0).astype(jnp.int32) + 2 * (s < strips - 1).astype(jnp.int32)
    )

    def spread(ext, base, block):
        across = remote(
            block,
            ext.at[mine, pl.ds(pl.multiple_of(half * g, half), strip), :],
            base, base, sibling,
        )
        down, up = [], []
        for j in range(2):
            src = block.at[quarter * j : quarter * (j + 1)]
            part = pl.ds(pl.multiple_of(slab * g + quarter * j, quarter), quarter)
            down.append(
                remote(
                    src.at[:, 0:half, :], ext.at[part, 2 * half : 3 * half, :],
                    base + 1 + j, base + 1 + 2 * g + j, (v, strip_before, 1),
                )
            )
            up.append(
                remote(
                    src.at[:, half:strip, :], ext.at[part, 0:half, :],
                    base + 3 + j, base + 1 + 2 * g + j, (v, strip_after, 0),
                )
            )
        return across, down, up

    def spread_start(copies):
        across, down, up = copies

        @pl.when(s > 0)
        def _():
            for copy in down:
                copy.start()

        @pl.when(s < strips - 1)
        def _():
            for copy in up:
                copy.start()

        across.start()

    def across_arrive(ext, base):
        theirs = pl.ds(pl.multiple_of(slab * (1 - g), slab), slab)
        remote(
            ext.at[mine, pl.ds(lay, strip), :], ext.at[theirs, pl.ds(lay, strip), :],
            base, base, sibling,
        ).wait_recv()

    def spread_arrive(ext, base, c, j):
        part = pl.ds(c * slab + j * quarter, quarter)
        number = base + 1 + 2 * c + j

        @pl.when(jnp.logical_and(g == 0, s > 0))
        def _():
            remote(
                ext.at[part, half : 2 * half, :], ext.at[part, 0:half, :],
                number, number, sibling,
            ).wait_recv()

        @pl.when(jnp.logical_and(g == 1, s < strips - 1))
        def _():
            remote(
                ext.at[part, half : 2 * half, :], ext.at[part, 2 * half : 3 * half, :],
                number, number, sibling,
            ).wait_recv()

    def spread_sent(copies):
        across, down, up = copies
        across.wait_send()

        @pl.when(s > 0)
        def _():
            for copy in down:
                copy.wait_send()

        @pl.when(s < strips - 1)
        def _():
            for copy in up:
                copy.wait_send()

    est_copies = spread(first, 0, first.at[mine, pl.ds(lay, strip), :])
    spread_start(est_copies)
    view_copies = spread(vext, 5, views.at[0])
    quarter_here = pl.ds(pl.multiple_of(quarter * vb, quarter), quarter)
    mast_copy = remote(
        est.at[quarter_here, pl.ds(pl.multiple_of(half * (1 - g), half), half), :],
        mast, 10, 10, sibling,
    )

    @pl.when(g == va)
    def _():
        mast_copy.start()
        mast[...] = est[quarter_here, pl.ds(pl.multiple_of(half * g, half), half), :]

    x_forward, = band(kern, 2, [(width, width, 1, reach)])
    x_backward, = band(kern, 2, [(width, width, -1, reach)])
    high, low = split(x_forward)
    xfor[:, :width] = high
    xfor[:, width:] = low
    high, low = split(x_backward)
    xback[:width, :width] = high
    xback[:width, width:] = low
    xback[width:, :width] = high
    xback[width:, width:] = jnp.zeros((width, width), BF16)
    z_mats = band(kern, 0, [(planes, planes, -1, reach), (planes, planes, 1, reach)])
    r_mats = band(
        kern, 1, [(half, 3 * half, -1, reach - half), (half, 3 * half, 1, reach + half)]
    )
    for way in range(2):
        high, low = split(z_mats[way])
        zmat[way, :planes, :] = high
        zmat[way, planes:, :] = low
        high, low = split(r_mats[way])
        rmat[way, :half, :] = high
        rmat[way, half:, :] = low

    def piece(k, h):
        return pl.ds(pl.multiple_of(quarter * other_view(k) + group * h, group), group)

    def halo(ext, base, k, h):
        part = piece(k, h)
        src = ext.at[part, half : 2 * half, :]
        at = base + 4 * k + 2 * h
        return (
            remote(src, ext.at[part, 2 * half : 3 * half, :], at, at, before),
            remote(src, ext.at[part, 0:half, :], at + 1, at + 1, after),
        )

    def halo_start(copies):
        down, up = copies

        @pl.when(has_prev)
        def _():
            down.start()

        @pl.when(has_next)
        def _():
            up.start()

    def halo_arrive(copies):
        down, up = copies

        @pl.when(has_next)
        def _():
            down.wait_recv()

        @pl.when(has_prev)
        def _():
            up.wait_recv()

    def halo_sent(copies):
        down, up = copies

        @pl.when(has_prev)
        def _():
            down.wait_send()

        @pl.when(has_next)
        def _():
            up.wait_send()

    def along_rows(ext, way, plane):
        mat = rmat[way]
        parts = []
        for i in range(0, group, 2):
            both = dot(mat, jnp.concatenate([ext[plane + i], ext[plane + i + 1]], axis=1))
            both = both[:half] + both[half:]
            parts += [both[:, :width], both[:, width:]]
        return jnp.concatenate(parts, axis=0)

    def forward(ext, plane):
        both = dot(along_rows(ext, 0, plane).astype(BF16), xfor[...])
        mid[pl.ds(pl.multiple_of(plane * half, group * half), group * half), :] = (
            both[:, :width] + both[:, width:]
        )

    def backward(ext, plane):
        high, low = split(along_rows(ext, 1, plane))
        both = dot(jnp.concatenate([high, low], axis=1), xback[...])
        return both[:, :width] + both[:, width:]

    def loop(steps, body, wide=1):
        def step(i, carry):
            for n in range(wide):
                body(wide * i + n)
            return carry

        lax.fori_loop(0, steps // wide, step, 0)

    block = lax.div(q * half, BLOCK)
    weight = cov[block, 0, v].astype(F32)
    count = jnp.float32(0.0)
    for n in range(4):
        count = count + cov[block, 0, n].astype(F32)

    across_arrive(first, 0)
    for j in range(2):
        for c in range(2):
            spread_arrive(first, 0, c, j)
            if (j, c) == (1, 1):
                spread_start(view_copies)
            for h in range(quarter // group):
                forward(first, c * slab + j * quarter + group * h)

    lay_views.wait()
    across_arrive(vext, 5)
    blank = jnp.zeros((slab * half, width), F32)
    data[: slab * half, :] = blank
    data[(slab + planes) * half :, :] = blank
    row = lax.broadcasted_iota(jnp.int32, (half, 3 * half), 0)
    col = lax.broadcasted_iota(jnp.int32, (half, 3 * half), 1)
    pick_rows = (col == row + half + shifts[0, 1]).astype(F32).astype(BF16)
    row = lax.broadcasted_iota(jnp.int32, (width, width), 0)
    col = lax.broadcasted_iota(jnp.int32, (width, width), 1)
    pick_x = (row == col + shifts[0, 2]).astype(F32).astype(BF16)

    def window(plane):
        parts = []
        for j in range(0, group, 2):
            pair = jnp.concatenate([vext[plane + j], vext[plane + j + 1]], axis=1)
            both = dot(pick_rows, pair)
            parts += [both[:, :width], both[:, width:]]
        moved = dot(jnp.concatenate(parts, axis=0).astype(BF16), pick_x)
        data[(slab + plane) * half : (slab + plane + group) * half, :] = moved

    for j in range(2):
        for c in range(2):
            spread_arrive(vext, 5, c, j)
            for h in range(quarter // group):
                window(c * slab + j * quarter + group * h)

    shifted = (slab + shifts[0, 0]) * half

    def column(ref, y):
        return jnp.concatenate(
            [ref[pl.ds(y, planes, stride=half), :], ref[pl.ds(y + 1, planes, stride=half), :]],
            axis=1,
        )

    def along_planes(i):
        for j in range(0, 4, 2):
            y = 4 * i + j
            both = dot(zmat[0], column(mid, y).astype(BF16))
            predicted = both[:planes] + both[planes:]
            ratio = column(data, y + shifted) / (predicted + 0.05)
            both = dot(zmat[1], ratio.astype(BF16))
            both = both[:planes] + both[planes:]
            back[pl.ds(y, planes, stride=half), :] = both[:, :width]
            back[pl.ds(y + 1, planes, stride=half), :] = both[:, width:]

    pieces = group * half
    order = ((3, 0), (3, 1), (1, 0), (2, 1), (1, 1), (2, 0), (0, 0), (0, 1))
    halos, sends, results = [], [], []

    for step in range(ITERS):
        loop(half // 4, along_planes, 2)
        ext = bext.at[step]
        last = step == ITERS - 1
        copies = {}
        for k, h in order:
            part = piece(k, h)
            at = pl.multiple_of((quarter * other_view(k) + group * h) * half, pieces)
            ext[part, half : 2 * half, :] = (
                back[pl.ds(at, pieces), :].reshape(group, half, width).astype(BF16)
            )
            copies[k, h] = halo(ext, 11 + 16 * step, k, h)
            halo_start(copies[k, h])
        halos += list(copies.values())
        base = 59 + 6 * step
        sums = {}
        for k in (3, 1, 2):
            for h in range(2):
                n = h if k == 3 else 2 * k + h
                sums[k, h] = coded(
                    term.at[step, n], term_top.at[step, n],
                    inbox.at[step, n], inbox_top.at[step, n],
                    base + n, base + n, (other_view(1 + h if k == 3 else k), s, g),
                )
        sends += list(sums.values())
        for k, h in order:
            halo_arrive(copies[k, h])
            value = weight * backward(ext, quarter * other_view(k) + group * h)
            if k == 0:
                own[h] = value
                continue
            if (k, h) in ((1, 1), (2, 0)):
                sums[3, h].wait_recv()
                value = value + decode(inbox[step, h], inbox_top[step, h])
            n = h if k == 3 else 2 * k + h
            term[step, n], term_top[step, n] = encode(value)
            sums[k, h].start()
        if step == 0:

            @pl.when(g != va)
            def _():
                mast_copy.wait_recv()

        here = quarter * v
        ext = None if last else fext.at[step + 1]
        news, copies = {}, {}
        for h in range(2):
            sums[1, h].wait_recv()
            sums[2, h].wait_recv()
            total = own[h]
            for n in (2 + h, 4 + h):
                total = total + decode(inbox[step, n], inbox_top[step, n])
            at = slice(group * h, group * (h + 1))
            field = mast[at] * total.reshape(group, half, width) / count
            if last:
                fin[h], fin_top[h] = encode(field.reshape(pieces, width))
                n = 4 * vb + 2 * g + h
                copies = [
                    coded(
                        fin.at[h], fin_top.at[h], final.at[n], final_top.at[n],
                        77 + 2 * k + h, 77 + n, (other_view(k), s, va),
                    )
                    for k in range(3)
                ]
                copies[1].start()
                copies[2].start()
                sends += copies[1:]
                results.append(copies[0])

                @pl.when(g != va)
                def _():
                    results[-1].start()

                continue
            mast[at] = field
            part = piece(0, h)
            ext[part, half : 2 * half, :] = field.astype(BF16)
            src = ext.at[part, half : 2 * half, :]
            for k in (1, 2):
                at = 71 + 2 * (k - 1) + h
                sent = remote(src, src, at, at, (other_view(k), s, g))
                sent.start()
                sends.append(sent)
            copies[0, h] = halo(ext, 43, 0, h)
            halo_start(copies[0, h])
        if last:
            break

        def gathered(k, h):
            src = ext.at[piece(k, h), half : 2 * half, :]
            at = 71 + 2 * (k - 1) + h
            remote(src, src, at, at, sibling).wait_recv()
            if (k, h) in ((1, 0), (2, 1)):
                sent = remote(src, src, 75 + h, 75 + h, (other_view(3 - k), s, g))
                sent.start()
                sends.append(sent)
            copies[k, h] = halo(ext, 43, k, h)
            halo_start(copies[k, h])

        def blurred(k, h):
            halo_arrive(copies[k, h])
            forward(ext, quarter * other_view(k) + group * h)

        for k, h in ((1, 0), (2, 0), (1, 1), (2, 1)):
            gathered(k, h)
        blurred(0, 0)
        blurred(0, 1)
        gathered(3, 0)
        blurred(1, 0)
        blurred(2, 0)
        gathered(3, 1)
        for k, h in ((1, 1), (2, 1), (3, 0), (3, 1)):
            blurred(k, h)
        halos += list(copies.values())

    same = 1 - lax.rem(g + va, 2)
    from_b = lax.rem(vb + same, 2)
    from_h = 1 - same
    onward = 2 * lax.rem(va + same, 2) + lax.rem(vb + 1 - same, 2)

    for c in range(2):
        n = 4 * from_b + 2 * c + from_h
        sent = coded(
            final.at[n], final_top.at[n], final.at[n], final_top.at[n],
            83 + c, 77 + n, (onward, s, g),
        )
        sent.wait_recv()
        sent.start()
        sends.append(sent)
    for h in range(2):
        for b in range(2):
            for c in range(2):
                n = 4 * b + 2 * c + h
                itself = jnp.logical_and(v == 2 * g + b, g == c)
                done = jnp.logical_and(from_b == b, from_h == h)

                def place(code, top):
                    first_plane = quarter * b + group * h
                    out[first_plane : first_plane + group, half * c : half * (c + 1), :] = decode(
                        code, top
                    ).reshape(group, half, width)

                @pl.when(jnp.logical_not(jnp.logical_or(itself, done)))
                def _():
                    coded(
                        final.at[n], final_top.at[n], final.at[n], final_top.at[n],
                        77 + n, 77 + n, sibling,
                    ).wait_recv()

                @pl.when(itself)
                def _():
                    place(fin[h], fin_top[h])

                @pl.when(jnp.logical_not(itself))
                def _():
                    place(final[n], final_top[n])

    @pl.when(g == va)
    def _():
        mast_copy.wait_send()

    @pl.when(g != va)
    def _():
        for copy in results:
            copy.wait_send()

    spread_sent(est_copies)
    spread_sent(view_copies)
    for copies in halos:
        halo_sent(copies)
    for sent in sends:
        sent.wait_send()


def on_device(strips, estimate, views, shifts, kernels, coverage):
    slab, strip, width = estimate.shape
    half, planes = strip // 2, 2 * slab
    quarter = planes // 4
    hbm = pl.BlockSpec(memory_space=pltpu.HBM)
    smem = pl.BlockSpec(memory_space=pltpu.SMEM)
    rows = planes * half
    scratch = [
        pltpu.VMEM(estimate.shape, F32),
        pltpu.VMEM((ITERS, planes, 3 * half, width), BF16),
        pltpu.VMEM((ITERS, planes, 3 * half, width), BF16),
        pltpu.VMEM((planes, 3 * half, width), BF16),
        pltpu.VMEM((2 * rows, width), F32),
        pltpu.VMEM((rows, width), F32),
        pltpu.VMEM((rows, width), F32),
        pltpu.VMEM((quarter, half, width), F32),
        pltpu.VMEM((2, quarter * half // 2, width), F32),
        pltpu.VMEM((ITERS, 6, quarter * half // 2, width), jnp.int16),
        pltpu.VMEM((ITERS, 6, 8, width), F32),
        pltpu.VMEM((ITERS, 6, quarter * half // 2, width), jnp.int16),
        pltpu.VMEM((ITERS, 6, 8, width), F32),
        pltpu.VMEM((2, quarter * half // 2, width), jnp.int16),
        pltpu.VMEM((2, 8, width), F32),
        pltpu.VMEM((8, quarter * half // 2, width), jnp.int16),
        pltpu.VMEM((8, 8, width), F32),
        pltpu.VMEM((2, 2 * half, 3 * half), BF16),
        pltpu.VMEM((width, 2 * width), BF16),
        pltpu.VMEM((2 * width, 2 * width), BF16),
        pltpu.VMEM((2, 2 * planes, planes), BF16),
        pltpu.SemaphoreType.DMA((85,)),
        pltpu.SemaphoreType.DMA((85,)),
        pltpu.SemaphoreType.DMA((85,)),
        pltpu.SemaphoreType.DMA((85,)),
        pltpu.SemaphoreType.DMA((2,)),
    ]
    return pl.pallas_call(
        functools.partial(kernel, strips),
        out_shape=jax.ShapeDtypeStruct(estimate.shape, F32),
        in_specs=[smem, smem, smem, hbm, hbm],
        out_specs=pl.BlockSpec(memory_space=pltpu.VMEM),
        scratch_shapes=scratch,
        compiler_params=pltpu.CompilerParams(
            collective_id=0, has_side_effects=True, vmem_limit_bytes=56 * 1024 * 1024
        ),
        cost_estimate=pl.CostEstimate(
            flops=12 * 2 * rows * width * 100, bytes_accessed=8 * rows * width, transcendentals=0
        ),
    )(coverage.transpose(1, 2, 0), shifts, kernels.transpose(1, 0, 2), estimate, views)


def solution(mesh):
    placed = (
        P("gz", "xy", None),
        P("view", "gz", "xy", None),
        P("view", None),
        P("view", None, None),
        P(),
    )
    return jax.shard_map(
        functools.partial(on_device, mesh.shape["xy"]),
        mesh=mesh, in_specs=placed, out_specs=P("gz", "xy", None), check_vma=False,
    )
```

```python
import functools

import jax
import jax.numpy as jnp
from jax import lax
from jax.experimental import pallas as pl
from jax.experimental.pallas import tpu as pltpu
from jax.sharding import PartitionSpec as P

BLOCK = 128
ITERS = 2
MESH = pl.DeviceIdType.MESH
F32 = jnp.float32
BF16 = jnp.bfloat16


def split(value):
    high = value.astype(BF16)
    return high, (value - high.astype(F32)).astype(BF16)


def encode(value):
    groups = value.reshape(-1, 8, value.shape[-1])
    top = jnp.maximum(jnp.max(groups, axis=0), 1e-30)
    whole = (groups * (32767.0 / top)[None] + 0.5).astype(jnp.int32)
    return whole.reshape(value.shape).astype(jnp.int16), top


def decode(code, top):
    groups = code.astype(jnp.int32).astype(F32).reshape(-1, 8, code.shape[-1])
    return (groups * (top * (1.0 / 32767.0))[None]).reshape(code.shape)


class Pair:
    def __init__(self, *copies):
        self.copies = copies

    def start(self):
        for copy in self.copies:
            copy.start()

    def wait_recv(self):
        for copy in self.copies:
            copy.wait_recv()

    def wait_send(self):
        for copy in self.copies:
            copy.wait_send()


def dot(a, b):
    return jnp.dot(a, b, preferred_element_type=F32)


def band(kern, axis, forms):
    marks = []
    for rows, cols, sign, base in forms:
        row = lax.broadcasted_iota(jnp.int32, (rows, cols), 0)
        col = lax.broadcasted_iota(jnp.int32, (rows, cols), 1)
        marks.append(base + sign * (row - col))

    def add_tap(tap, carry):
        total, mats = carry
        value = kern[axis, 0, tap]
        return total + value, tuple(
            mat + jnp.where(mark == tap, value, 0.0) for mat, mark in zip(mats, marks)
        )

    zeros = tuple(jnp.zeros(mark.shape, F32) for mark in marks)
    total, mats = lax.fori_loop(0, kern.shape[2], add_tap, (jnp.float32(0.0), zeros))
    return [mat / total for mat in mats]


def kernel(
    strips, cov, shifts, kern, given, views, out,
    est, fext, bext, vext, data, mid, back, mast, own, term, term_top, inbox, inbox_top,
    fin, fin_top, final, final_top,
    rmat, xfor, xback, zmat, send, recv, send_top, recv_top, local,
):
    slab, strip, width = est.shape
    half = strip // 2
    planes = 2 * slab
    taps = kern.shape[2]
    reach = (taps - 1) // 2
    quarter = planes // 4
    group = quarter // 2
    pitch = half + 8
    v, s, g = lax.axis_index("view"), lax.axis_index("xy"), lax.axis_index("gz")
    va, vb = lax.div(v, 2), lax.rem(v, 2)
    q = 2 * s + g
    has_prev, has_next = q > 0, q < 2 * strips - 1

    def other_view(k):
        return lax.rem(va + k // 2, 2) * 2 + lax.rem(vb + k % 2, 2)

    fetch = pltpu.make_async_copy(given, est, local.at[0])
    fetch.start()
    sibling = (v, s, 1 - g)
    before = (v, lax.rem(s - 1 + g + strips, strips), 1 - g)
    after = (v, lax.rem(s + g, strips), 1 - g)
    strip_before = lax.rem(s - 1 + strips, strips)
    strip_after = lax.rem(s + 1, strips)

    barrier = pltpu.get_barrier_semaphore()

    def greet(device):
        pl.semaphore_signal(barrier, inc=1, device_id=device, device_id_type=MESH)

    greet(sibling)
    for k in range(1, 4):
        greet((other_view(k), s, g))
        greet((other_view(k), s, 1 - g))

    @pl.when(s > 0)
    def _():
        greet((v, strip_before, 0))
        greet((v, strip_before, 1))

    @pl.when(s < strips - 1)
    def _():
        greet((v, strip_after, 0))
        greet((v, strip_after, 1))

    def remote(src, dst, send_id, recv_id, device):
        return pltpu.make_async_remote_copy(
            src_ref=src, dst_ref=dst, send_sem=send.at[send_id], recv_sem=recv.at[recv_id],
            device_id=device, device_id_type=MESH,
        )

    def coded(src, src_top, dst, dst_top, send_id, recv_id, device):
        return Pair(
            remote(src, dst, send_id, recv_id, device),
            pltpu.make_async_remote_copy(
                src_ref=src_top, dst_ref=dst_top, send_sem=send_top.at[send_id],
                recv_sem=recv_top.at[recv_id], device_id=device, device_id_type=MESH,
            ),
        )

    mine = pl.ds(pl.multiple_of(slab * g, slab), slab)
    lay = pl.multiple_of(half - half * g, half)
    first = fext.at[0]

    lay_views = pltpu.make_async_copy(
        views.at[0], vext.at[mine, pl.ds(lay, strip), :], local.at[1]
    )
    lay_views.start()

    @pl.when(q == 0)
    def _():
        vext[:, 0:half, :] = jnp.zeros((planes, half, width), BF16)
        for n in range(ITERS):
            fext[n, :, 0:half, :] = jnp.zeros((planes, half, width), BF16)
            bext[n, :, 0:half, :] = jnp.zeros((planes, half, width), BF16)

    @pl.when(q == 2 * strips - 1)
    def _():
        vext[:, 2 * half :, :] = jnp.zeros((planes, half, width), BF16)
        for n in range(ITERS):
            fext[n, :, 2 * half :, :] = jnp.zeros((planes, half, width), BF16)
            bext[n, :, 2 * half :, :] = jnp.zeros((planes, half, width), BF16)

    fetch.wait()
    for i in range(0, slab, group):
        first[pl.ds(slab * g + i, group), pl.ds(lay, strip), :] = est[i : i + group].astype(BF16)

    pl.semaphore_wait(
        barrier, 7 + 2 * (s > 0).astype(jnp.int32) + 2 * (s < strips - 1).astype(jnp.int32)
    )

    def spread(ext, base, block):
        across = remote(
            block,
            ext.at[mine, pl.ds(pl.multiple_of(half * g, half), strip), :],
            base, base, sibling,
        )
        down, up = [], []
        for j in range(2):
            src = block.at[quarter * j : quarter * (j + 1)]
            part = pl.ds(pl.multiple_of(slab * g + quarter * j, quarter), quarter)
            down.append(
                remote(
                    src.at[:, 0:half, :], ext.at[part, 2 * half : 3 * half, :],
                    base + 1 + j, base + 1 + 2 * g + j, (v, strip_before, 1),
                )
            )
            up.append(
                remote(
                    src.at[:, half:strip, :], ext.at[part, 0:half, :],
                    base + 3 + j, base + 1 + 2 * g + j, (v, strip_after, 0),
                )
            )
        return across, down, up

    def spread_start(copies):
        across, down, up = copies

        @pl.when(s > 0)
        def _():
            for copy in down:
                copy.start()

        @pl.when(s < strips - 1)
        def _():
            for copy in up:
                copy.start()

        across.start()

    def across_arrive(ext, base):
        theirs = pl.ds(pl.multiple_of(slab * (1 - g), slab), slab)
        remote(
            ext.at[mine, pl.ds(lay, strip), :], ext.at[theirs, pl.ds(lay, strip), :],
            base, base, sibling,
        ).wait_recv()

    def spread_arrive(ext, base, c, j):
        part = pl.ds(c * slab + j * quarter, quarter)
        number = base + 1 + 2 * c + j

        @pl.when(jnp.logical_and(g == 0, s > 0))
        def _():
            remote(
                ext.at[part, half : 2 * half, :], ext.at[part, 0:half, :],
                number, number, sibling,
            ).wait_recv()

        @pl.when(jnp.logical_and(g == 1, s < strips - 1))
        def _():
            remote(
                ext.at[part, half : 2 * half, :], ext.at[part, 2 * half : 3 * half, :],
                number, number, sibling,
            ).wait_recv()

    def spread_sent(copies):
        across, down, up = copies
        across.wait_send()

        @pl.when(s > 0)
        def _():
            for copy in down:
                copy.wait_send()

        @pl.when(s < strips - 1)
        def _():
            for copy in up:
                copy.wait_send()

    est_copies = spread(first, 0, first.at[mine, pl.ds(lay, strip), :])
    spread_start(est_copies)
    view_copies = spread(vext, 5, views.at[0])
    quarter_here = pl.ds(pl.multiple_of(quarter * vb, quarter), quarter)
    mast_copy = remote(
        est.at[quarter_here, pl.ds(pl.multiple_of(half * (1 - g), half), half), :],
        mast, 10, 10, sibling,
    )

    @pl.when(g == va)
    def _():
        mast_copy.start()
        mast[...] = est[quarter_here, pl.ds(pl.multiple_of(half * g, half), half), :]

    x_forward, = band(kern, 2, [(width, width, 1, reach)])
    x_backward, = band(kern, 2, [(width, width, -1, reach)])
    high, low = split(x_forward)
    xfor[:, :width] = high
    xfor[:, width:] = low
    high, low = split(x_backward)
    xback[:width, :width] = high
    xback[:width, width:] = low
    xback[width:, :width] = high
    xback[width:, width:] = jnp.zeros((width, width), BF16)
    z_mats = band(kern, 0, [(planes, planes, -1, reach), (planes, planes, 1, reach)])
    r_mats = band(
        kern, 1, [(half, 3 * half, -1, reach - half), (half, 3 * half, 1, reach + half)]
    )
    for way in range(2):
        high, low = split(z_mats[way])
        zmat[way, :planes, :] = high
        zmat[way, planes:, :] = low
        high, low = split(r_mats[way])
        rmat[way, :half, :] = high
        rmat[way, half:, :] = low

    def piece(k, h):
        return pl.ds(pl.multiple_of(quarter * other_view(k) + group * h, group), group)

    def halo(ext, base, k, h):
        part = piece(k, h)
        src = ext.at[part, half : 2 * half, :]
        at = base + 4 * k + 2 * h
        return (
            remote(src, ext.at[part, 2 * half : 3 * half, :], at, at, before),
            remote(src, ext.at[part, 0:half, :], at + 1, at + 1, after),
        )

    def halo_start(copies):
        down, up = copies

        @pl.when(has_prev)
        def _():
            down.start()

        @pl.when(has_next)
        def _():
            up.start()

    def halo_arrive(copies):
        down, up = copies

        @pl.when(has_next)
        def _():
            down.wait_recv()

        @pl.when(has_prev)
        def _():
            up.wait_recv()

    def halo_sent(copies):
        down, up = copies

        @pl.when(has_prev)
        def _():
            down.wait_send()

        @pl.when(has_next)
        def _():
            up.wait_send()

    def along_rows(ext, way, plane):
        mat = rmat[way]
        parts = []
        for i in range(0, group, 2):
            both = dot(mat, jnp.concatenate([ext[plane + i], ext[plane + i + 1]], axis=1))
            both = both[:half] + both[half:]
            parts += [both[:, :width], both[:, width:]]
        return jnp.concatenate(parts, axis=0)

    def forward(ext, plane):
        both = dot(along_rows(ext, 0, plane).astype(BF16), xfor[...])
        both = both[:, :width] + both[:, width:]
        for i in range(group):
            at = pl.multiple_of((plane + i) * pitch, 8)
            mid[pl.ds(at, half), :] = both[half * i : half * (i + 1)]

    def backward(ext, plane):
        high, low = split(along_rows(ext, 1, plane))
        both = dot(jnp.concatenate([high, low], axis=1), xback[...])
        return both[:, :width] + both[:, width:]

    def loop(steps, body, wide=1):
        def step(i, carry):
            for n in range(wide):
                body(wide * i + n)
            return carry

        lax.fori_loop(0, steps // wide, step, 0)

    block = lax.div(q * half, BLOCK)
    weight = cov[block, 0, v].astype(F32)
    count = jnp.float32(0.0)
    for n in range(4):
        count = count + cov[block, 0, n].astype(F32)

    across_arrive(first, 0)
    for j in range(2):
        for c in range(2):
            spread_arrive(first, 0, c, j)
            if (j, c) == (1, 1):
                spread_start(view_copies)
            for h in range(quarter // group):
                forward(first, c * slab + j * quarter + group * h)

    lay_views.wait()
    across_arrive(vext, 5)
    blank = jnp.zeros((slab * pitch, width), F32)
    data[: slab * pitch, :] = blank
    data[(slab + planes) * pitch :, :] = blank
    row = lax.broadcasted_iota(jnp.int32, (half, 3 * half), 0)
    col = lax.broadcasted_iota(jnp.int32, (half, 3 * half), 1)
    pick_rows = (col == row + half + shifts[0, 1]).astype(F32).astype(BF16)
    row = lax.broadcasted_iota(jnp.int32, (width, width), 0)
    col = lax.broadcasted_iota(jnp.int32, (width, width), 1)
    pick_x = (row == col + shifts[0, 2]).astype(F32).astype(BF16)

    def window(plane):
        parts = []
        for j in range(0, group, 2):
            pair = jnp.concatenate([vext[plane + j], vext[plane + j + 1]], axis=1)
            both = dot(pick_rows, pair)
            parts += [both[:, :width], both[:, width:]]
        moved = dot(jnp.concatenate(parts, axis=0).astype(BF16), pick_x)
        for i in range(group):
            at = (slab + plane + i) * pitch
            data[at : at + half, :] = moved[half * i : half * (i + 1)]

    for j in range(2):
        for c in range(2):
            spread_arrive(vext, 5, c, j)
            for h in range(quarter // group):
                window(c * slab + j * quarter + group * h)

    shifted = (slab + shifts[0, 0]) * pitch

    def column(ref, y):
        return jnp.concatenate(
            [ref[pl.ds(y, planes, stride=pitch), :], ref[pl.ds(y + 1, planes, stride=pitch), :]],
            axis=1,
        )

    def along_planes(i):
        for j in range(0, 4, 2):
            y = 4 * i + j
            both = dot(zmat[0], column(mid, y).astype(BF16))
            predicted = both[:planes] + both[planes:]
            ratio = column(data, y + shifted) / (predicted + 0.05)
            both = dot(zmat[1], ratio.astype(BF16))
            both = both[:planes] + both[planes:]
            back[pl.ds(y, planes, stride=pitch), :] = both[:, :width]
            back[pl.ds(y + 1, planes, stride=pitch), :] = both[:, width:]

    pieces = group * half
    order = ((3, 0), (3, 1), (1, 0), (2, 1), (1, 1), (2, 0), (0, 0), (0, 1))
    halos, sends, results = [], [], []

    for step in range(ITERS):
        loop(half // 4, along_planes, 2)
        ext = bext.at[step]
        last = step == ITERS - 1
        copies = {}
        for k, h in order:
            start = quarter * other_view(k) + group * h
            for i in range(group):
                at = pl.multiple_of((start + i) * pitch, 8)
                ext[start + i, half : 2 * half, :] = back[pl.ds(at, half), :].astype(BF16)
            copies[k, h] = halo(ext, 11 + 16 * step, k, h)
            halo_start(copies[k, h])
        halos += list(copies.values())
        base = 59 + 6 * step
        sums = {}
        for k in (3, 1, 2):
            for h in range(2):
                n = h if k == 3 else 2 * k + h
                sums[k, h] = coded(
                    term.at[step, n], term_top.at[step, n],
                    inbox.at[step, n], inbox_top.at[step, n],
                    base + n, base + n, (other_view(1 + h if k == 3 else k), s, g),
                )
        sends += list(sums.values())
        for k, h in order:
            halo_arrive(copies[k, h])
            value = weight * backward(ext, quarter * other_view(k) + group * h)
            if k == 0:
                own[h] = value
                continue
            if (k, h) in ((1, 1), (2, 0)):
                sums[3, h].wait_recv()
                value = value + decode(inbox[step, h], inbox_top[step, h])
            n = h if k == 3 else 2 * k + h
            term[step, n], term_top[step, n] = encode(value)
            sums[k, h].start()
        if step == 0:

            @pl.when(g != va)
            def _():
                mast_copy.wait_recv()

        here = quarter * v
        ext = None if last else fext.at[step + 1]
        news, copies = {}, {}
        for h in range(2):
            sums[1, h].wait_recv()
            sums[2, h].wait_recv()
            total = own[h]
            for n in (2 + h, 4 + h):
                total = total + decode(inbox[step, n], inbox_top[step, n])
            at = slice(group * h, group * (h + 1))
            field = mast[at] * total.reshape(group, half, width) / count
            if last:
                fin[h], fin_top[h] = encode(field.reshape(pieces, width))
                n = 4 * vb + 2 * g + h
                copies = [
                    coded(
                        fin.at[h], fin_top.at[h], final.at[n], final_top.at[n],
                        77 + 2 * k + h, 77 + n, (other_view(k), s, va),
                    )
                    for k in range(3)
                ]
                copies[1].start()
                copies[2].start()
                sends += copies[1:]
                results.append(copies[0])

                @pl.when(g != va)
                def _():
                    results[-1].start()

                continue
            mast[at] = field
            part = piece(0, h)
            ext[part, half : 2 * half, :] = field.astype(BF16)
            src = ext.at[part, half : 2 * half, :]
            for k in (1, 2):
                at = 71 + 2 * (k - 1) + h
                sent = remote(src, src, at, at, (other_view(k), s, g))
                sent.start()
                sends.append(sent)
            copies[0, h] = halo(ext, 43, 0, h)
            halo_start(copies[0, h])
        if last:
            break

        def gathered(k, h):
            src = ext.at[piece(k, h), half : 2 * half, :]
            at = 71 + 2 * (k - 1) + h
            remote(src, src, at, at, sibling).wait_recv()
            if (k, h) in ((1, 0), (2, 1)):
                sent = remote(src, src, 75 + h, 75 + h, (other_view(3 - k), s, g))
                sent.start()
                sends.append(sent)
            copies[k, h] = halo(ext, 43, k, h)
            halo_start(copies[k, h])

        def blurred(k, h):
            halo_arrive(copies[k, h])
            forward(ext, quarter * other_view(k) + group * h)

        for k, h in ((1, 0), (2, 0), (1, 1), (2, 1)):
            gathered(k, h)
        blurred(0, 0)
        blurred(0, 1)
        gathered(3, 0)
        blurred(1, 0)
        blurred(2, 0)
        gathered(3, 1)
        for k, h in ((1, 1), (2, 1), (3, 0), (3, 1)):
            blurred(k, h)
        halos += list(copies.values())

    same = 1 - lax.rem(g + va, 2)
    from_b = lax.rem(vb + same, 2)
    from_h = 1 - same
    onward = 2 * lax.rem(va + same, 2) + lax.rem(vb + 1 - same, 2)

    for c in range(2):
        n = 4 * from_b + 2 * c + from_h
        sent = coded(
            final.at[n], final_top.at[n], final.at[n], final_top.at[n],
            83 + c, 77 + n, (onward, s, g),
        )
        sent.wait_recv()
        sent.start()
        sends.append(sent)
    for h in range(2):
        for b in range(2):
            for c in range(2):
                n = 4 * b + 2 * c + h
                itself = jnp.logical_and(v == 2 * g + b, g == c)
                done = jnp.logical_and(from_b == b, from_h == h)

                def place(code, top):
                    first_plane = quarter * b + group * h
                    out[first_plane : first_plane + group, half * c : half * (c + 1), :] = decode(
                        code, top
                    ).reshape(group, half, width)

                @pl.when(jnp.logical_not(jnp.logical_or(itself, done)))
                def _():
                    coded(
                        final.at[n], final_top.at[n], final.at[n], final_top.at[n],
                        77 + n, 77 + n, sibling,
                    ).wait_recv()

                @pl.when(itself)
                def _():
                    place(fin[h], fin_top[h])

                @pl.when(jnp.logical_not(itself))
                def _():
                    place(final[n], final_top[n])

    @pl.when(g == va)
    def _():
        mast_copy.wait_send()

    @pl.when(g != va)
    def _():
        for copy in results:
            copy.wait_send()

    spread_sent(est_copies)
    spread_sent(view_copies)
    for copies in halos:
        halo_sent(copies)
    for sent in sends:
        sent.wait_send()


def on_device(strips, estimate, views, shifts, kernels, coverage):
    slab, strip, width = estimate.shape
    half, planes = strip // 2, 2 * slab
    quarter = planes // 4
    hbm = pl.BlockSpec(memory_space=pltpu.HBM)
    smem = pl.BlockSpec(memory_space=pltpu.SMEM)
    rows = planes * half
    scratch = [
        pltpu.VMEM(estimate.shape, F32),
        pltpu.VMEM((ITERS, planes, 3 * half, width), BF16),
        pltpu.VMEM((ITERS, planes, 3 * half, width), BF16),
        pltpu.VMEM((planes, 3 * half, width), BF16),
        pltpu.VMEM((2 * planes * (half + 8), width), F32),
        pltpu.VMEM((planes * (half + 8), width), F32),
        pltpu.VMEM((planes * (half + 8), width), F32),
        pltpu.VMEM((quarter, half, width), F32),
        pltpu.VMEM((2, quarter * half // 2, width), F32),
        pltpu.VMEM((ITERS, 6, quarter * half // 2, width), jnp.int16),
        pltpu.VMEM((ITERS, 6, 8, width), F32),
        pltpu.VMEM((ITERS, 6, quarter * half // 2, width), jnp.int16),
        pltpu.VMEM((ITERS, 6, 8, width), F32),
        pltpu.VMEM((2, quarter * half // 2, width), jnp.int16),
        pltpu.VMEM((2, 8, width), F32),
        pltpu.VMEM((8, quarter * half // 2, width), jnp.int16),
        pltpu.VMEM((8, 8, width), F32),
        pltpu.VMEM((2, 2 * half, 3 * half), BF16),
        pltpu.VMEM((width, 2 * width), BF16),
        pltpu.VMEM((2 * width, 2 * width), BF16),
        pltpu.VMEM((2, 2 * planes, planes), BF16),
        pltpu.SemaphoreType.DMA((85,)),
        pltpu.SemaphoreType.DMA((85,)),
        pltpu.SemaphoreType.DMA((85,)),
        pltpu.SemaphoreType.DMA((85,)),
        pltpu.SemaphoreType.DMA((2,)),
    ]
    return pl.pallas_call(
        functools.partial(kernel, strips),
        out_shape=jax.ShapeDtypeStruct(estimate.shape, F32),
        in_specs=[smem, smem, smem, hbm, hbm],
        out_specs=pl.BlockSpec(memory_space=pltpu.VMEM),
        scratch_shapes=scratch,
        compiler_params=pltpu.CompilerParams(
            collective_id=0, has_side_effects=True, vmem_limit_bytes=40 * 1024 * 1024
        ),
        cost_estimate=pl.CostEstimate(
            flops=12 * 2 * rows * width * 100, bytes_accessed=8 * rows * width, transcendentals=0
        ),
    )(coverage.transpose(1, 2, 0), shifts, kernels.transpose(1, 0, 2), estimate, views)


def solution(mesh):
    placed = (
        P("gz", "xy", None),
        P("view", "gz", "xy", None),
        P("view", None),
        P("view", None, None),
        P(),
    )
    return jax.shard_map(
        functools.partial(on_device, mesh.shape["xy"]),
        mesh=mesh, in_specs=placed, out_specs=P("gz", "xy", None), check_vma=False,
    )
```
